32 devices in a mesh: grp: 4 (over x, core), row: 4 (over z), col: 2 (over y).
Axes of the slice: x: 2, y: 2, z: 4, core: 2. Of those that a mesh axis runs over, the one named last changes fastest.
Arguments:
- tokens_in: bfloat16 [256, 6144], P('col', 'row'), may hold values from -6 to 6
- cotangent: bfloat16 [256, 6144], P('col', 'grp'), may hold values from -6 to 6
- sample_rows: int32 [64], P('col'), may hold values from 0 to 255, as said below
- act_inverse: bfloat16 [6144, 6144], P('grp', 'row'), as said below
- grad_inverse: bfloat16 [6144, 6144], P('grp', 'col'), as said below
Outputs:
- precond: float32 [6144, 6144], P(('grp', 'row'), 'col')
- act_cov: float32 [6144, 6144], P(('row', 'col'), 'grp')
- grad_cov: float32 [6144, 6144], P(('row', 'col'), 'grp')
The draws below stay inside these ranges and needn't reach their ends.
Inputs may be any that keep to these rules, and one draw needn't show every extreme that they name: `sample_rows`: for each block c, entries c * 32 to (c + 1) * 32 - 1 are distinct token rows of that block, between c * 128 and (c + 1) * 128 - 1. `act_inverse`: Symmetric. `grad_inverse`: Symmetric.
All inputs are finite; a program needn't handle non-finite values.
Results may differ from the reference program's by a relative error of at most 0.03.
Values may be sent and summed in bfloat16 or wider, within the bound.
A program may use at most 128 MiB of HBM per device.

```python
import jax
import jax.numpy as jnp
from jax import lax

D = 6144
TOK_DEV = 128
SAMP_DEV = 32
TOKENS = 256
SAMPLES = 64
N_ROW = 4


def inverse_factor(key, spread):
    noise = jax.random.normal(jax.random.fold_in(key, 11), (D, D), jnp.float32)
    mixed = (noise + noise.T) * (spread / D ** 0.5)
    level = jnp.exp(jax.random.uniform(jax.random.fold_in(key, 12), (D,), jnp.float32, -0.7, 0.7))
    return (mixed + jnp.diag(level)).astype(jnp.bfloat16)


def draw_act_inverse(key, part):
    key = jax.random.fold_in(key, 1)
    return inverse_factor(key, 0.35)


def draw_grad_inverse(key, part):
    key = jax.random.fold_in(key, 2)
    return inverse_factor(key, 0.3)


def draw_sample_rows(key, part):
    key = jax.random.fold_in(key, 3)
    count = TOKENS // TOK_DEV
    keys = jax.random.split(key, count)
    orders = jax.vmap(lambda k: jax.random.permutation(k, TOK_DEV))(keys)[:, :SAMP_DEV]
    blocks = jnp.arange(count, dtype=jnp.int32)
    target = jnp.where(blocks == 0, 0, jnp.where(blocks == count - 1, TOK_DEV - 1, orders[:, 0]))
    shifted = (orders - orders[:, :1] + target[:, None] + TOK_DEV) % TOK_DEV
    return (shifted + blocks[:, None] * TOK_DEV).reshape(count * SAMP_DEV).astype(jnp.int32)


def level_of(rng, extent, cuts, low, largest):
    gain, own = 1.0, jax.random.fold_in(rng, 6)
    for dim, blocks in cuts:
        heights = jnp.exp(jax.random.uniform(jax.random.fold_in(own, dim), (blocks,), jnp.float32, low / len(cuts), largest / len(cuts)))
        gain = gain * jnp.repeat(heights, extent[dim] // blocks).reshape([-1 if axis == dim else 1 for axis in range(len(extent))])
    return gain


def scatter_about(own_key, shape, deviation, limit, cuts=(), kind=jnp.bfloat16):
    gain = level_of(own_key, shape, cuts, -0.22, 0.18) if cuts else 1.0
    result = jax.random.normal(own_key, shape, jnp.float32) * deviation * gain
    return jnp.minimum(jnp.maximum(result, -limit), limit).astype(kind)


def setup_inputs(seed: int = 0) -> dict:
    arg_keys = jax.random.split(jax.random.key(seed), 6)
    return {
        "tokens_in": scatter_about(arg_keys[0], (TOKENS, D), 1.0, 6.0, ((0, 2), (1, 4))),
        "cotangent": scatter_about(arg_keys[1], (TOKENS, D), 1.0, 6.0, ((0, 2), (1, 4))),
        "sample_rows": draw_sample_rows(jax.random.fold_in(arg_keys[5], 71), 0),
        "act_inverse": draw_act_inverse(jax.random.fold_in(arg_keys[5], 71), 0),
        "grad_inverse": draw_grad_inverse(jax.random.fold_in(arg_keys[5], 71), 0),
    }


def reference(tokens_in, cotangent, sample_rows, act_inverse, grad_inverse):
    blocks_x = tokens_in.reshape(TOKENS // TOK_DEV, TOK_DEV, D)
    blocks_g = cotangent.reshape(TOKENS // TOK_DEV, TOK_DEV, D)

    def grad_step(total, pair):
        part = lax.dot_general(pair[0], pair[1], (((0,), (0,)), ((), ())), preferred_element_type=jnp.float32)
        part = lax.optimization_barrier(part.astype(jnp.bfloat16)).astype(jnp.float32)
        return total + part, None

    summed, unused = lax.scan(grad_step, jnp.zeros((D, D), jnp.float32), (blocks_x, blocks_g))
    grad_weight = summed.astype(jnp.bfloat16)
    right = jnp.dot(grad_weight, grad_inverse, preferred_element_type=jnp.float32).astype(jnp.bfloat16)
    inner = D // N_ROW

    def left_step(total, block):
        begin = block.astype(jnp.int32) * inner
        cols = lax.dynamic_slice_in_dim(act_inverse, begin, inner, 1)
        rows = lax.dynamic_slice_in_dim(right, begin, inner, 0)
        part = jnp.dot(cols, rows, preferred_element_type=jnp.float32)
        part = lax.optimization_barrier(part.astype(jnp.bfloat16)).astype(jnp.float32)
        return total + part, None

    precond, unused = lax.scan(left_step, jnp.zeros((D, D), jnp.float32), jnp.arange(N_ROW, dtype=jnp.int32))
    picked_x = jnp.take(tokens_in, sample_rows, axis=0)
    picked_g = jnp.take(cotangent, sample_rows, axis=0)
    dims = (((0,), (0,)), ((), ()))
    act_cov = lax.dot_general(picked_x, picked_x, dims, preferred_element_type=jnp.float32) / SAMPLES
    grad_cov = lax.dot_general(picked_g, picked_g, dims, preferred_element_type=jnp.float32) / SAMPLES
    return precond, act_cov, grad_cov
```

```python
import jax
import jax.numpy as jnp
from jax import lax
from jax.sharding import PartitionSpec as P

SHRINK = 2.0 ** -16


def body(tokens_in, cotangent, sample_rows, act_inverse, grad_inverse):
    feat_row = tokens_in.shape[1]
    feat_grp = cotangent.shape[1]
    n_row = lax.axis_size("row")
    n_col = lax.axis_size("col")
    n_grp = lax.axis_size("grp")
    width = feat_row * n_row
    contract = (((0,), (0,)), ((), ()))
    col_index = lax.axis_index("col")
    grp_index = lax.axis_index("grp")
    row_index = lax.axis_index("row")
    small = tokens_in * jnp.asarray(SHRINK, tokens_in.dtype)
    part_u = lax.dot_general(
        small, act_inverse, (((1,), (1,)), ((), ())), preferred_element_type=jnp.float32
    )
    u = lax.psum_scatter(part_u.astype(jnp.bfloat16), "row", scatter_dimension=1, tiled=True)
    u = lax.all_gather(u, "col", axis=0, tiled=True)
    all_cot = lax.all_gather(cotangent, "col", axis=0, tiled=True)
    share = grad_inverse.shape[1] // n_row
    mine = lax.dynamic_slice_in_dim(grad_inverse, row_index * share, share, 1)
    part_v = jnp.dot(all_cot, mine, preferred_element_type=jnp.float32)
    v = lax.psum(part_v.astype(jnp.bfloat16), "grp")
    v = lax.all_gather(v, "row", axis=1, tiled=True)
    precond = lax.dot_general(u, v, contract, preferred_element_type=jnp.float32) * (1 / SHRINK)
    offsets = sample_rows - col_index * tokens_in.shape[0]
    picked_x = jnp.take(tokens_in, offsets, axis=0)
    picked_g = jnp.take(cotangent, offsets, axis=0)
    samples = picked_x.shape[0]
    total = samples * n_col
    act_panel = lax.all_gather(picked_x[None], ("row", "col"), axis=0, tiled=True).reshape(
        n_row, total, feat_row
    )
    grad_panel = lax.all_gather(picked_g[None], ("grp", "col"), axis=0, tiled=True).reshape(
        n_grp, total, feat_grp
    )
    tile = width // (n_row * n_col)
    first = (row_index * n_col + col_index) * tile
    act_left = lax.dynamic_slice(
        act_panel, (first // feat_row, 0, first % feat_row), (1, total, tile)
    )[0]
    per = feat_grp // feat_row
    act_span = lax.dynamic_slice_in_dim(act_panel, grp_index * per, per, 0)
    act_cov = jnp.einsum("sa,psf->apf", act_left, act_span, preferred_element_type=jnp.float32)
    act_cov = act_cov.reshape(tile, feat_grp) / total
    grad_left = lax.dynamic_slice(
        grad_panel, (first // feat_grp, 0, first % feat_grp), (1, total, tile)
    )[0]
    grad_span = lax.dynamic_index_in_dim(grad_panel, grp_index, 0, keepdims=False)
    grad_cov = (
        lax.dot_general(grad_left, grad_span, contract, preferred_element_type=jnp.float32) / total
    )
    return (precond, act_cov, grad_cov)


def solution(mesh):
    return jax.shard_map(
        body,
        mesh=mesh,
        in_specs=(P("col", "row"), P("col", "grp"), P("col"), P("grp", "row"), P("grp", "col")),
        out_specs=(P(("grp", "row"), "col"), P(("row", "col"), "grp"), P(("row", "col"), "grp")),
        check_vma=False,
    )
```

```python
import functools

import jax
import jax.numpy as jnp
from jax import lax
from jax.experimental import pallas as pl
from jax.experimental.pallas import tpu as pltpu
from jax.sharding import PartitionSpec as P

SHRINK = 2.0 ** -16
BF16 = jnp.bfloat16
F32 = jnp.float32
CONTRACT = (((0,), (0,)), ((), ()))


def gather_kernel(
    rows_ref, t_hbm, c_hbm, a_hbm, g_hbm,
    u_out, v_out, xl_out, xs_out, yl_out, ys_out,
    t_v, c_v, a_v, g_v, oh_v, px_v, q_v, r1_s, r1_r, r2_s, r2_r,
    w_s, w_r, w_v, h_s, h_r, u_v, v_v, xl_v, xs_v, yl_v, ys_v,
    load_sem, out_sem, send_sem, recv_sem,
):
    grp, z, c = lax.axis_index("grp"), lax.axis_index("row"), lax.axis_index("col")
    x, k = grp // 2, grp % 2
    oc, ok, ox = 1 - c, 1 - k, 1 - x
    z1 = z + 1 - 2 * (z % 2)
    z2 = (z + 2) % 4
    z3 = (z1 + 2) % 4
    to_y = {"col": oc}
    to_k = {"grp": 2 * x + ok}
    to_x = {"grp": 2 * ox + k}
    to_xk = {"grp": 2 * ox + ok}
    to_z1 = {"row": z1}
    to_z2 = {"row": z2}
    tok = t_v.shape[0]
    feat = t_v.shape[1]
    share = g_v.shape[1]
    half = xl_v.shape[2]
    out_rows = u_v.shape[2]
    piece = tok // 4

    names = {}

    def copy(name, src, dst, where):
        i = names.setdefault(name, len(names))
        return pltpu.make_async_remote_copy(
            src_ref=src, dst_ref=dst, send_sem=send_sem.at[i], recv_sem=recv_sem.at[i],
            device_id=where, device_id_type=pl.DeviceIdType.MESH,
        )

    loads = [
        pltpu.make_async_copy(c_hbm, c_v.at[c], load_sem.at[0]),
        pltpu.make_async_copy(
            g_hbm.at[:, pl.ds(pl.multiple_of(z * share, 128), share)], g_v, load_sem.at[1]
        ),
        pltpu.make_async_copy(t_hbm, t_v, load_sem.at[2]),
        pltpu.make_async_copy(a_hbm, a_v, load_sem.at[3]),
    ]
    for load in loads:
        load.start()

    barrier = pltpu.get_barrier_semaphore()
    partners = [to_y, to_k, to_x, to_xk, to_z1, to_z2]
    for where in partners:
        pl.semaphore_signal(barrier, inc=1, device_id=where, device_id_type=pl.DeviceIdType.MESH)
    pl.semaphore_wait(barrier, len(partners))

    cot = copy("cot", c_hbm, c_v.at[c], to_y)
    cot_in = copy("cot", c_hbm, c_v.at[oc], to_y)
    cot.start()

    hot = (rows_ref[...] == lax.broadcasted_iota(jnp.int32, (rows_ref.shape[0], tok), 1))
    hot = jnp.where(hot, 1.0, 0.0).astype(BF16)
    oh_v[c] = hot
    hot_out = copy("hot", oh_v.at[c], oh_v.at[c], to_y)
    hot_in = copy("hot", oh_v.at[oc], oh_v.at[oc], to_y)
    hot_out.start()
    sends = [cot, hot_out]

    def v_at(block, core, side, zz):
        row = pl.multiple_of(block * tok + core * (2 * piece) + side * piece, piece)
        return v_v.at[pl.ds(row, piece), pl.ds(pl.multiple_of(zz * share, 128), share)]

    def send(name, src, dst, where):
        out = copy(name, src, dst, where)
        out.start()
        sends.append(out)

    def await_in(name, dst, where):
        copy(name, dst, dst, where).wait_recv()

    def product(ph, block):
        q = jnp.dot(c_v[block], g_v[...], preferred_element_type=F32)
        q_v[ph] = q.reshape(4, piece, share)
        r1_s[ph] = q_v[ph, pl.ds(2 * ok, 2)].astype(BF16)
        send(("r1", ph), r1_s.at[ph], r1_r.at[ph], to_k)

    def across(ph):
        await_in(("r1", ph), r1_r.at[ph], to_k)
        r2_s[ph] = (q_v[ph, 2 * k + ox] + r1_r[ph, ox].astype(F32)).astype(BF16)
        send(("r2", ph), r2_s.at[ph], r2_r.at[ph], to_x)

    def finish(ph, block):
        await_in(("r2", ph), r2_r.at[ph], to_x)
        total = q_v[ph, 2 * k + x] + r1_r[ph, x].astype(F32) + r2_r[ph].astype(F32)
        mine = v_at(block, k, x, z)
        mine[...] = total.astype(BF16)
        send(("v2", ph), mine, mine, to_z2)
        send(("v1", ph), mine, mine, to_z1)
        send(("vx", ph, 0), mine, mine, to_x)
        send(("vk", ph, 0), mine, mine, to_k)

    def spread(ph, block, step):
        zz = (z, z2, z1, z3)[step]
        got = v_at(block, k, x, zz)
        await_in((("v0", "v2", "v1", "v3")[step], ph), got, to_z1)
        if step == 1:
            send(("v3", ph), got, got, to_z1)
        send(("vx", ph, step), got, got, to_x)
        send(("vk", ph, step), got, got, to_k)

    def relay(ph, block, step):
        zz = (z, z2, z1, z3)[step]
        got = v_at(block, k, ox, zz)
        await_in(("vx", ph, step), got, to_x)
        send(("vk", ph, 4 + step), got, got, to_k)

    def collect(ph, block):
        for step in range(4):
            zz = (z, z2, z1, z3)[step]
            await_in(("vk", ph, step), v_at(block, ok, x, zz), to_k)
        for step in range(4):
            zz = (z, z2, z1, z3)[step]
            await_in(("vk", ph, 4 + step), v_at(block, ok, ox, zz), to_k)

    def u_part(block):
        rows = a_v[pl.ds(pl.multiple_of(block * out_rows, out_rows), out_rows), :]
        return lax.dot_general(t_v[...], rows, (((1,), (1,)), ((), ())), preferred_element_type=F32)

    def at_half(ref, index):
        return ref.at[:, pl.ds(pl.multiple_of(index * half, 128), half)]

    loads[0].wait()
    loads[1].wait()
    product(0, c)

    loads[2].wait()
    px_v[...] = jnp.dot(hot, t_v[...], preferred_element_type=F32).astype(BF16)
    send("xl", at_half(px_v, oc), xl_v.at[c], to_y)
    xl_v[c] = at_half(px_v, c)[...]
    has_span = grp == z
    span = xs_v.at[c]

    @pl.when(has_span)
    def _():
        xs_v[c] = px_v[...]

    x_z2 = copy("x2", span, span, to_z2)
    x_z1 = copy("x1", span, span, to_z1)
    x_y = copy("xy", span, span, to_y)

    @pl.when(has_span)
    def _():
        x_z2.start()
        x_z1.start()

    ys_v[c] = jnp.dot(hot, c_v[c], preferred_element_type=F32).astype(BF16)
    across(0)

    t_v[...] = t_v[...] * jnp.asarray(SHRINK, BF16)
    loads[3].wait()
    other = 1 - z % 2
    for i in range(2):
        w_s[i] = u_part(other + 2 * i).astype(BF16)
    send("w", w_s, w_r, to_z1)
    finish(0, c)
    for i in range(2):
        w_v[i] = u_part(z % 2 + 2 * i)

    is_z2 = grp == z2
    is_z1 = grp == z1

    @pl.when(is_z2)
    def _():
        x_z2.wait_recv()
        x_z1.start()

    await_in("w", w_r, to_z1)
    mine, away = z // 2, 1 - z // 2
    h_s[...] = (w_v[away] + w_r[away].astype(F32)).astype(BF16)
    send("h", h_s, h_r, to_z2)
    spread(0, c, 1)
    spread(0, c, 2)

    @pl.when(jnp.logical_or(is_z1, grp == z3))
    def _():
        x_z1.wait_recv()

    x_y.start()
    sends.append(x_y)
    await_in("h", h_r, to_z2)
    u_v[c] = (w_v[mine] + w_r[mine].astype(F32) + h_r[...].astype(F32)).astype(BF16)
    send("u", u_v.at[c], u_v.at[c], to_y)
    spread(0, c, 3)

    cot_in.wait_recv()
    product(1, oc)
    hot_in.wait_recv()
    ys_v[oc] = jnp.dot(oh_v[oc], c_v[oc], preferred_element_type=F32).astype(BF16)
    left = ys_v.at[:, :, pl.ds(pl.multiple_of(c * half, 128), half)]
    y_outs = [copy(("yl", i), left, yl_v, w) for i, w in enumerate([to_k, to_x, to_xk])]

    @pl.when(has_span)
    def _():
        for out in y_outs:
            out.start()
        yl_v[...] = left[...]

    across(1)
    for step in range(4):
        relay(0, c, step)
    finish(1, oc)
    for step in range(1, 4):
        spread(1, oc, step)
    collect(0, c)

    outs = [pltpu.make_async_copy(
        v_v.at[pl.ds(pl.multiple_of(c * tok, tok), tok)],
        v_out.at[pl.ds(pl.multiple_of(c * tok, tok), tok)], out_sem.at[0])]
    outs[0].start()
    await_in("xl", xl_v.at[oc], to_y)
    await_in("xy", xs_v.at[oc], to_y)
    await_in("u", u_v.at[oc], to_y)
    for i, (src, dst) in enumerate([(u_v, u_out), (xl_v, xl_out), (xs_v, xs_out), (ys_v, ys_out)]):
        out = pltpu.make_async_copy(src, dst, out_sem.at[2 + i])
        out.start()
        outs.append(out)

    @pl.when(grp == 2 * (z // 2) + (1 - z % 2))
    def _():
        y_outs[0].wait_recv()

    @pl.when(grp == 2 * (1 - z // 2) + z % 2)
    def _():
        y_outs[1].wait_recv()

    @pl.when(grp == 2 * (1 - z // 2) + (1 - z % 2))
    def _():
        y_outs[2].wait_recv()

    out = pltpu.make_async_copy(yl_v, yl_out, out_sem.at[6])
    out.start()
    outs.append(out)
    for step in range(4):
        relay(1, oc, step)
    collect(1, oc)
    out = pltpu.make_async_copy(
        v_v.at[pl.ds(pl.multiple_of(oc * tok, tok), tok)],
        v_out.at[pl.ds(pl.multiple_of(oc * tok, tok), tok)], out_sem.at[1])
    out.start()
    outs.append(out)

    @pl.when(has_span)
    def _():
        x_z2.wait_send()
        x_z1.wait_send()
        for out in y_outs:
            out.wait_send()

    @pl.when(is_z2)
    def _():
        x_z1.wait_send()

    for out in sends:
        out.wait_send()
    for out in outs:
        out.wait()


def gather(rows, tokens_in, cotangent, act_inverse, grad_inverse, n_row):
    tok, feat = tokens_in.shape
    samples = rows.shape[0]
    share = grad_inverse.shape[1] // n_row
    out_rows = feat // n_row
    half = feat // 2
    piece = tok // 4
    shapes = [
        (2, tok, out_rows), (2 * tok, grad_inverse.shape[1]),
        (2, samples, half), (2, samples, feat), (2, samples, half), (2, samples, feat),
    ]
    vmem = pltpu.VMEM
    return pl.pallas_call(
        gather_kernel,
        out_shape=[jax.ShapeDtypeStruct(s, BF16) for s in shapes],
        in_specs=[pl.BlockSpec(memory_space=vmem)] + [pl.BlockSpec(memory_space=pl.ANY)] * 4,
        out_specs=[pl.BlockSpec(memory_space=pl.ANY)] * 6,
        scratch_shapes=[
            vmem((tok, feat), BF16),
            vmem((2, tok, feat), BF16),
            vmem(act_inverse.shape, BF16),
            vmem((feat, share), BF16),
            vmem((2, samples, tok), BF16),
            vmem((samples, feat), BF16),
            vmem((2, 4, piece, share), F32),
            vmem((2, 2, piece, share), BF16),
            vmem((2, 2, piece, share), BF16),
            vmem((2, piece, share), BF16),
            vmem((2, piece, share), BF16),
            vmem((2, tok, out_rows), BF16),
            vmem((2, tok, out_rows), BF16),
            vmem((2, tok, out_rows), F32),
            vmem((tok, out_rows), BF16),
            vmem((tok, out_rows), BF16),
        ] + [vmem(s, BF16) for s in shapes] + [
            pltpu.SemaphoreType.DMA((4,)),
            pltpu.SemaphoreType.DMA((7,)),
            pltpu.SemaphoreType.DMA((48,)),
            pltpu.SemaphoreType.DMA((48,)),
        ],
        compiler_params=pltpu.CompilerParams(
            collective_id=0, has_side_effects=True, vmem_limit_bytes=40 * 2 ** 20
        ),
        cost_estimate=pl.CostEstimate(flops=3 * 10 ** 9, bytes_accessed=10 ** 7, transcendentals=0),
    )(rows, tokens_in, cotangent, act_inverse, grad_inverse)


def product_kernel(total, u, v, xl, xs, yl, ys, p_out, a_out, g_out, ut, xt, yt):
    @pl.when(pl.program_id(0) == 0)
    def _():
        ut[...] = u[...].T
        xt[...] = xl[...].T
        yt[...] = yl[...].T

    a_out[...] = jnp.dot(xt[...], xs[...], preferred_element_type=F32) * (1 / total)
    g_out[...] = jnp.dot(yt[...], ys[...], preferred_element_type=F32) * (1 / total)
    p_out[...] = jnp.dot(ut[...], v[...], preferred_element_type=F32) * (1 / SHRINK)


def products(u, v, xl, xs, yl, ys):
    steps = 6
    total = xl.shape[0]

    def whole(a):
        return pl.BlockSpec(a.shape, lambda i: (0, 0))

    def cut(rows, width):
        return pl.BlockSpec((rows, width // steps), lambda i: (0, i))

    return pl.pallas_call(
        functools.partial(product_kernel, total),
        grid=(steps,),
        in_specs=[
            whole(u), cut(v.shape[0], v.shape[1]),
            whole(xl), cut(total, xs.shape[1]), whole(yl), cut(total, ys.shape[1]),
        ],
        out_specs=[
            cut(u.shape[1], v.shape[1]), cut(xl.shape[1], xs.shape[1]), cut(yl.shape[1], ys.shape[1])
        ],
        out_shape=[
            jax.ShapeDtypeStruct((u.shape[1], v.shape[1]), F32),
            jax.ShapeDtypeStruct((xl.shape[1], xs.shape[1]), F32),
            jax.ShapeDtypeStruct((yl.shape[1], ys.shape[1]), F32),
        ],
        scratch_shapes=[
            pltpu.VMEM(u.shape[::-1], BF16), pltpu.VMEM(xl.shape[::-1], BF16),
            pltpu.VMEM(yl.shape[::-1], BF16),
        ],
        compiler_params=pltpu.CompilerParams(vmem_limit_bytes=40 * 2 ** 20),
        cost_estimate=pl.CostEstimate(flops=10 ** 9, bytes_accessed=17 * 10 ** 6, transcendentals=0),
    )(u, v, xl, xs, yl, ys)


def flat(a):
    return a.reshape(-1, a.shape[-1])


def body_kernels(tokens_in, cotangent, sample_rows, act_inverse, grad_inverse):
    rows = (sample_rows - lax.axis_index("col") * tokens_in.shape[0])[:, None]
    u, v, xl, xs, yl, ys = gather(
        rows, tokens_in, cotangent, act_inverse, grad_inverse, lax.axis_size("row")
    )
    return tuple(products(flat(u), v, flat(xl), flat(xs), flat(yl), flat(ys)))


def body(tokens_in, cotangent, sample_rows, act_inverse, grad_inverse):
    feat_row = tokens_in.shape[1]
    feat_grp = cotangent.shape[1]
    n_row = lax.axis_size("row")
    n_col = lax.axis_size("col")
    n_grp = lax.axis_size("grp")
    width = feat_row * n_row
    contract = (((0,), (0,)), ((), ()))
    col_index = lax.axis_index("col")
    grp_index = lax.axis_index("grp")
    row_index = lax.axis_index("row")
    small = tokens_in * jnp.asarray(SHRINK, tokens_in.dtype)
    part_u = lax.dot_general(
        small, act_inverse, (((1,), (1,)), ((), ())), preferred_element_type=jnp.float32
    )
    u = lax.psum_scatter(part_u.astype(jnp.bfloat16), "row", scatter_dimension=1, tiled=True)
    u = lax.all_gather(u, "col", axis=0, tiled=True)
    all_cot = lax.all_gather(cotangent, "col", axis=0, tiled=True)
    share = grad_inverse.shape[1] // n_row
    mine = lax.dynamic_slice_in_dim(grad_inverse, row_index * share, share, 1)
    part_v = jnp.dot(all_cot, mine, preferred_element_type=jnp.float32)
    v = lax.psum(part_v.astype(jnp.bfloat16), "grp")
    v = lax.all_gather(v, "row", axis=1, tiled=True)
    precond = lax.dot_general(u, v, contract, preferred_element_type=jnp.float32) * (1 / SHRINK)
    offsets = sample_rows - col_index * tokens_in.shape[0]
    picked_x = jnp.take(tokens_in, offsets, axis=0)
    picked_g = jnp.take(cotangent, offsets, axis=0)
    samples = picked_x.shape[0]
    total = samples * n_col
    act_panel = lax.all_gather(picked_x[None], ("row", "col"), axis=0, tiled=True).reshape(
        n_row, total, feat_row
    )
    grad_panel = lax.all_gather(picked_g[None], ("grp", "col"), axis=0, tiled=True).reshape(
        n_grp, total, feat_grp
    )
    tile = width // (n_row * n_col)
    first = (row_index * n_col + col_index) * tile
    act_left = lax.dynamic_slice(
        act_panel, (first // feat_row, 0, first % feat_row), (1, total, tile)
    )[0]
    per = feat_grp // feat_row
    act_span = lax.dynamic_slice_in_dim(act_panel, grp_index * per, per, 0)
    act_cov = jnp.einsum("sa,psf->apf", act_left, act_span, preferred_element_type=jnp.float32)
    act_cov = act_cov.reshape(tile, feat_grp) / total
    grad_left = lax.dynamic_slice(
        grad_panel, (first // feat_grp, 0, first % feat_grp), (1, total, tile)
    )[0]
    grad_span = lax.dynamic_index_in_dim(grad_panel, grp_index, 0, keepdims=False)
    grad_cov = (
        lax.dot_general(grad_left, grad_span, contract, preferred_element_type=jnp.float32) / total
    )
    return (precond, act_cov, grad_cov)


def solution(mesh):
    sizes = tuple(mesh.shape[name] for name in ("grp", "row", "col"))
    return jax.shard_map(
        body_kernels if sizes == (4, 4, 2) else body,
        mesh=mesh,
        in_specs=(P("col", "row"), P("col", "grp"), P("col"), P("grp", "row"), P("grp", "col")),
        out_specs=(P(("grp", "row"), "col"), P(("row", "col"), "grp"), P(("row", "col"), "grp")),
        check_vma=False,
    )
```

```python
import functools

import jax
import jax.numpy as jnp
from jax import lax
from jax.experimental import pallas as pl
from jax.experimental.pallas import tpu as pltpu
from jax.sharding import PartitionSpec as P

SHRINK = 2.0 ** -16
BF16 = jnp.bfloat16
F32 = jnp.float32
CONTRACT = (((0,), (0,)), ((), ()))


def gather_kernel(
    rows_ref, t_hbm, c_hbm, a_hbm, g_hbm,
    u_out, v_out, xl_out, xs_out, yl_out, ys_out,
    t_v, c_v, a_v, g_v, oh_v, px_v, q_v, r1_s, r1_r, r2_s, r2_r,
    w_s, w_r, w_v, h_s, h_r, u_v, v_v, xl_v, xs_v, yl_v, ys_v,
    load_sem, out_sem, send_sem, recv_sem,
):
    grp, z, c = lax.axis_index("grp"), lax.axis_index("row"), lax.axis_index("col")
    x, k = grp // 2, grp % 2
    oc, ok, ox = 1 - c, 1 - k, 1 - x
    z1 = z + 1 - 2 * (z % 2)
    z2 = (z + 2) % 4
    z3 = (z1 + 2) % 4
    places = (z, z2, z1, z3)
    to_y = {"col": oc}
    to_k = {"grp": 2 * x + ok}
    to_x = {"grp": 2 * ox + k}
    to_xk = {"grp": 2 * ox + ok}
    to_z1 = {"row": z1}
    to_z2 = {"row": z2}
    tok = t_v.shape[0]
    share = g_v.shape[1]
    half = xl_v.shape[2]
    out_rows = u_v.shape[2]
    phases = ((c, 0, tok), (oc, 0, tok // 2), (oc, tok // 2, tok // 2))

    names = {}
    sends = []

    def copy(name, src, dst, where):
        i = names.setdefault(name, len(names))
        return pltpu.make_async_remote_copy(
            src_ref=src, dst_ref=dst, send_sem=send_sem.at[i], recv_sem=recv_sem.at[i],
            device_id=where, device_id_type=pl.DeviceIdType.MESH,
        )

    def send(name, src, dst, where):
        out = copy(name, src, dst, where)
        out.start()
        sends.append(out)

    def await_in(name, dst, where):
        copy(name, dst, dst, where).wait_recv()

    loads = [
        pltpu.make_async_copy(c_hbm, c_v.at[c], load_sem.at[0]),
        pltpu.make_async_copy(
            g_hbm.at[:, pl.ds(pl.multiple_of(z * share, 128), share)], g_v, load_sem.at[1]
        ),
        pltpu.make_async_copy(t_hbm, t_v, load_sem.at[2]),
        pltpu.make_async_copy(a_hbm, a_v, load_sem.at[3]),
    ]
    for load in loads:
        load.start()

    barrier = pltpu.get_barrier_semaphore()
    partners = [to_y, to_k, to_x, to_xk, to_z1, to_z2]
    for where in partners:
        pl.semaphore_signal(barrier, inc=1, device_id=where, device_id_type=pl.DeviceIdType.MESH)
    pl.semaphore_wait(barrier, len(partners))

    for ph in (1, 2):
        part = pl.ds(phases[ph][1], phases[ph][2])
        send(("cot", ph), c_hbm.at[part], c_v.at[c, part], to_y)

    hot = lax.broadcasted_iota(jnp.int32, (tok, rows_ref.shape[1]), 0) + c * tok == rows_ref[...]
    oh_v[c] = jnp.where(hot, 1.0, 0.0).astype(BF16)
    send("hot", oh_v.at[c], oh_v.at[c], to_y)

    def pick(block, values):
        return lax.dot_general(oh_v[block], values, CONTRACT, preferred_element_type=F32).astype(BF16)

    def v_at(ph, core, side, step):
        block, first, count = phases[ph]
        row = pl.multiple_of(block * tok + first + (2 * core + side) * (count // 4), count // 4)
        return v_v.at[
            pl.ds(row, count // 4), pl.ds(pl.multiple_of(places[step] * share, 128), share)
        ]

    def cut(ph):
        return pl.ds(0, phases[ph][2] // 4)

    def product(ph):
        block, first, count = phases[ph]
        q = jnp.dot(c_v[block, first:first + count], g_v[...], preferred_element_type=F32)
        q_v[ph, :, cut(ph)] = q.reshape(4, count // 4, share)
        r1_s[ph, :, cut(ph)] = q_v[ph, pl.ds(2 * ok, 2), cut(ph)].astype(BF16)
        send(("r1", ph), r1_s.at[ph, :, cut(ph)], r1_r.at[ph, :, cut(ph)], to_k)

    def across(ph):
        await_in(("r1", ph), r1_r.at[ph, :, cut(ph)], to_k)
        r2_s[ph, cut(ph)] = (
            q_v[ph, 2 * k + ox, cut(ph)] + r1_r[ph, ox, cut(ph)].astype(F32)
        ).astype(BF16)
        send(("r2", ph), r2_s.at[ph, cut(ph)], r2_r.at[ph, cut(ph)], to_x)

    def finish(ph):
        await_in(("r2", ph), r2_r.at[ph, cut(ph)], to_x)
        total = (
            q_v[ph, 2 * k + x, cut(ph)] + r1_r[ph, x, cut(ph)].astype(F32)
            + r2_r[ph, cut(ph)].astype(F32)
        )
        mine = v_at(ph, k, x, 0)
        mine[...] = total.astype(BF16)
        send(("v", ph, 1), mine, mine, to_z2)
        send(("v", ph, 2), mine, mine, to_z1)
        send(("vx", ph, 0), mine, mine, to_x)
        send(("vk", ph, 0), mine, mine, to_k)

    def spread(ph, step):
        got = v_at(ph, k, x, step)
        await_in(("v", ph, step), got, to_z1)
        if step == 1:
            send(("v", ph, 3), got, got, to_z1)
        send(("vx", ph, step), got, got, to_x)
        send(("vk", ph, step), got, got, to_k)

    def relay(ph, step):
        got = v_at(ph, k, ox, step)
        await_in(("vx", ph, step), got, to_x)
        send(("vk", ph, 4 + step), got, got, to_k)

    def collect(ph):
        for step in range(4):
            await_in(("vk", ph, step), v_at(ph, ok, x, step), to_k)
        for step in range(4):
            await_in(("vk", ph, 4 + step), v_at(ph, ok, ox, step), to_k)

    def u_part(block):
        rows = a_v[pl.ds(pl.multiple_of(block * out_rows, out_rows), out_rows), :]
        return lax.dot_general(t_v[...], rows, (((1,), (1,)), ((), ())), preferred_element_type=F32)

    def at_half(ref, index):
        return ref.at[:, pl.ds(pl.multiple_of(index * half, 128), half)]

    def await_cot(ph):
        part = pl.ds(phases[ph][1], phases[ph][2])
        await_in(("cot", ph), c_v.at[oc, part], to_y)

    has_span = grp == z
    is_z2 = grp == z2
    is_z1 = grp == z1
    span = xs_v.at[c]
    x_z2 = copy("x2", span, span, to_z2)
    x_z1 = copy("x1", span, span, to_z1)

    loads[0].wait()
    loads[1].wait()
    product(0)
    loads[2].wait()
    px_v[...] = pick(c, t_v[...])
    t_v[...] = t_v[...] * jnp.asarray(SHRINK, BF16)
    ys_v[c] = pick(c, c_v[c])
    across(0)

    loads[3].wait()
    for i in range(2):
        w_s[i] = u_part(1 - z % 2 + 2 * i).astype(BF16)
    send("w", w_s, w_r, to_z1)

    @pl.when(has_span)
    def _():
        xs_v[c] = px_v[...]
        x_z2.start()
        x_z1.start()

    finish(0)
    await_cot(1)
    product(1)
    for i in range(2):
        w_v[i] = u_part(z % 2 + 2 * i)
    across(1)
    finish(1)
    spread(0, 1)
    spread(0, 2)
    await_cot(2)
    product(2)
    send("xl", at_half(px_v, oc), xl_v.at[c], to_y)
    xl_v[c] = at_half(px_v, c)[...]
    await_in("w", w_r, to_z1)
    mine, away = z // 2, 1 - z // 2
    h_s[...] = (w_v[away] + w_r[away].astype(F32)).astype(BF16)
    send("h", h_s, h_r, to_z2)
    across(2)
    spread(0, 3)
    spread(1, 1)
    spread(1, 2)
    finish(2)

    @pl.when(is_z2)
    def _():
        x_z2.wait_recv()
        x_z1.start()

    await_in("hot", oh_v.at[oc], to_y)
    ys_v[oc] = pick(oc, c_v[oc])
    left = ys_v.at[:, :, pl.ds(pl.multiple_of(c * half, 128), half)]
    y_outs = [copy(("yl", i), left, yl_v, w) for i, w in enumerate([to_k, to_x, to_xk])]

    @pl.when(has_span)
    def _():
        for out in y_outs:
            out.start()
        yl_v[...] = left[...]

    for step in range(4):
        relay(0, step)
    spread(1, 3)

    @pl.when(jnp.logical_or(is_z1, grp == z3))
    def _():
        x_z1.wait_recv()

    send("xy", span, span, to_y)
    await_in("h", h_r, to_z2)
    u_v[c] = (w_v[mine] + w_r[mine].astype(F32) + h_r[...].astype(F32)).astype(BF16)
    send("u", u_v.at[c], u_v.at[c], to_y)
    for step in range(1, 4):
        spread(2, step)
    for step in range(4):
        relay(1, step)
    for step in range(4):
        relay(2, step)
    collect(0)

    outs = []

    def put(src, dst):
        out = pltpu.make_async_copy(src, dst, out_sem.at[len(outs)])
        out.start()
        outs.append(out)

    def put_v(ph):
        block, first, count = phases[ph]
        rows = pl.ds(pl.multiple_of(block * tok + first, count), count)
        put(v_v.at[rows], v_out.at[rows])

    put_v(0)
    put(ys_v, ys_out)
    collect(1)
    put_v(1)
    await_in("xl", xl_v.at[oc], to_y)
    put(xl_v, xl_out)

    @pl.when(grp == 2 * (z // 2) + (1 - z % 2))
    def _():
        y_outs[0].wait_recv()

    @pl.when(grp == 2 * (1 - z // 2) + z % 2)
    def _():
        y_outs[1].wait_recv()

    @pl.when(grp == 2 * (1 - z // 2) + (1 - z % 2))
    def _():
        y_outs[2].wait_recv()

    put(yl_v, yl_out)
    await_in("xy", xs_v.at[oc], to_y)
    put(xs_v, xs_out)
    await_in("u", u_v.at[oc], to_y)
    put(u_v, u_out)
    collect(2)
    put_v(2)

    @pl.when(has_span)
    def _():
        x_z2.wait_send()
        x_z1.wait_send()
        for out in y_outs:
            out.wait_send()

    @pl.when(is_z2)
    def _():
        x_z1.wait_send()

    for out in sends:
        out.wait_send()
    for out in outs:
        out.wait()


def gather(rows, tokens_in, cotangent, act_inverse, grad_inverse, n_row):
    tok, feat = tokens_in.shape
    samples = rows.shape[1]
    share = grad_inverse.shape[1] // n_row
    out_rows = feat // n_row
    half = feat // 2
    piece = tok // 4
    shapes = [
        (2, tok, out_rows), (2 * tok, grad_inverse.shape[1]),
        (2, samples, half), (2, samples, feat), (2, samples, half), (2, samples, feat),
    ]
    vmem = pltpu.VMEM
    return pl.pallas_call(
        gather_kernel,
        out_shape=[jax.ShapeDtypeStruct(s, BF16) for s in shapes],
        in_specs=[pl.BlockSpec(memory_space=vmem)] + [pl.BlockSpec(memory_space=pl.ANY)] * 4,
        out_specs=[pl.BlockSpec(memory_space=pl.ANY)] * 6,
        scratch_shapes=[
            vmem((tok, feat), BF16),
            vmem((2, tok, feat), BF16),
            vmem(act_inverse.shape, BF16),
            vmem((feat, share), BF16),
            vmem((2, tok, samples), BF16),
            vmem((samples, feat), BF16),
            vmem((3, 4, piece, share), F32),
            vmem((3, 2, piece, share), BF16),
            vmem((3, 2, piece, share), BF16),
            vmem((3, piece, share), BF16),
            vmem((3, piece, share), BF16),
            vmem((2, tok, out_rows), BF16),
            vmem((2, tok, out_rows), BF16),
            vmem((2, tok, out_rows), F32),
            vmem((tok, out_rows), BF16),
            vmem((tok, out_rows), BF16),
        ] + [vmem(s, BF16) for s in shapes] + [
            pltpu.SemaphoreType.DMA((4,)),
            pltpu.SemaphoreType.DMA((8,)),
            pltpu.SemaphoreType.DMA((68,)),
            pltpu.SemaphoreType.DMA((68,)),
        ],
        compiler_params=pltpu.CompilerParams(
            collective_id=0, has_side_effects=True, vmem_limit_bytes=60 * 2 ** 20
        ),
        cost_estimate=pl.CostEstimate(flops=3 * 10 ** 9, bytes_accessed=10 ** 7, transcendentals=0),
    )(rows, tokens_in, cotangent, act_inverse, grad_inverse)


def product_kernel(total, u, v, xl, xs, yl, ys, p_out, a_out, g_out, ut, xt, yt):
    @pl.when(pl.program_id(0) == 0)
    def _():
        ut[...] = u[...].T
        xt[...] = xl[...].T
        yt[...] = yl[...].T

    a_out[...] = jnp.dot(xt[...], xs[...], preferred_element_type=F32) * (1 / total)
    g_out[...] = jnp.dot(yt[...], ys[...], preferred_element_type=F32) * (1 / total)
    p_out[...] = jnp.dot(ut[...], v[...], preferred_element_type=F32) * (1 / SHRINK)


def products(u, v, xl, xs, yl, ys):
    steps = 6
    total = xl.shape[0]

    def whole(a):
        return pl.BlockSpec(a.shape, lambda i: (0, 0))

    def cut(rows, width):
        return pl.BlockSpec((rows, width // steps), lambda i: (0, i))

    return pl.pallas_call(
        functools.partial(product_kernel, total),
        grid=(steps,),
        in_specs=[
            whole(u), cut(v.shape[0], v.shape[1]),
            whole(xl), cut(total, xs.shape[1]), whole(yl), cut(total, ys.shape[1]),
        ],
        out_specs=[
            cut(u.shape[1], v.shape[1]), cut(xl.shape[1], xs.shape[1]), cut(yl.shape[1], ys.shape[1])
        ],
        out_shape=[
            jax.ShapeDtypeStruct((u.shape[1], v.shape[1]), F32),
            jax.ShapeDtypeStruct((xl.shape[1], xs.shape[1]), F32),
            jax.ShapeDtypeStruct((yl.shape[1], ys.shape[1]), F32),
        ],
        scratch_shapes=[
            pltpu.VMEM(u.shape[::-1], BF16), pltpu.VMEM(xl.shape[::-1], BF16),
            pltpu.VMEM(yl.shape[::-1], BF16),
        ],
        compiler_params=pltpu.CompilerParams(vmem_limit_bytes=40 * 2 ** 20),
        cost_estimate=pl.CostEstimate(flops=10 ** 9, bytes_accessed=17 * 10 ** 6, transcendentals=0),
    )(u, v, xl, xs, yl, ys)


def flat(a):
    return a.reshape(-1, a.shape[-1])


def body_kernels(tokens_in, cotangent, sample_rows, act_inverse, grad_inverse):
    u, v, xl, xs, yl, ys = gather(
        sample_rows[None], tokens_in, cotangent, act_inverse, grad_inverse, lax.axis_size("row")
    )
    return tuple(products(flat(u), v, flat(xl), flat(xs), flat(yl), flat(ys)))


def body(tokens_in, cotangent, sample_rows, act_inverse, grad_inverse):
    feat_row = tokens_in.shape[1]
    feat_grp = cotangent.shape[1]
    n_row = lax.axis_size("row")
    n_col = lax.axis_size("col")
    n_grp = lax.axis_size("grp")
    width = feat_row * n_row
    contract = (((0,), (0,)), ((), ()))
    col_index = lax.axis_index("col")
    grp_index = lax.axis_index("grp")
    row_index = lax.axis_index("row")
    small = tokens_in * jnp.asarray(SHRINK, tokens_in.dtype)
    part_u = lax.dot_general(
        small, act_inverse, (((1,), (1,)), ((), ())), preferred_element_type=jnp.float32
    )
    u = lax.psum_scatter(part_u.astype(jnp.bfloat16), "row", scatter_dimension=1, tiled=True)
    u = lax.all_gather(u, "col", axis=0, tiled=True)
    all_cot = lax.all_gather(cotangent, "col", axis=0, tiled=True)
    share = grad_inverse.shape[1] // n_row
    mine = lax.dynamic_slice_in_dim(grad_inverse, row_index * share, share, 1)
    part_v = jnp.dot(all_cot, mine, preferred_element_type=jnp.float32)
    v = lax.psum(part_v.astype(jnp.bfloat16), "grp")
    v = lax.all_gather(v, "row", axis=1, tiled=True)
    precond = lax.dot_general(u, v, contract, preferred_element_type=jnp.float32) * (1 / SHRINK)
    offsets = sample_rows - col_index * tokens_in.shape[0]
    picked_x = jnp.take(tokens_in, offsets, axis=0)
    picked_g = jnp.take(cotangent, offsets, axis=0)
    samples = picked_x.shape[0]
    total = samples * n_col
    act_panel = lax.all_gather(picked_x[None], ("row", "col"), axis=0, tiled=True).reshape(
        n_row, total, feat_row
    )
    grad_panel = lax.all_gather(picked_g[None], ("grp", "col"), axis=0, tiled=True).reshape(
        n_grp, total, feat_grp
    )
    tile = width // (n_row * n_col)
    first = (row_index * n_col + col_index) * tile
    act_left = lax.dynamic_slice(
        act_panel, (first // feat_row, 0, first % feat_row), (1, total, tile)
    )[0]
    per = feat_grp // feat_row
    act_span = lax.dynamic_slice_in_dim(act_panel, grp_index * per, per, 0)
    act_cov = jnp.einsum("sa,psf->apf", act_left, act_span, preferred_element_type=jnp.float32)
    act_cov = act_cov.reshape(tile, feat_grp) / total
    grad_left = lax.dynamic_slice(
        grad_panel, (first // feat_grp, 0, first % feat_grp), (1, total, tile)
    )[0]
    grad_span = lax.dynamic_index_in_dim(grad_panel, grp_index, 0, keepdims=False)
    grad_cov = (
        lax.dot_general(grad_left, grad_span, contract, preferred_element_type=jnp.float32) / total
    )
    return (precond, act_cov, grad_cov)


def solution(mesh):
    sizes = tuple(mesh.shape[name] for name in ("grp", "row", "col"))
    return jax.shard_map(
        body_kernels if sizes == (4, 4, 2) else body,
        mesh=mesh,
        in_specs=(P("col", "row"), P("col", "grp"), P("col"), P("grp", "row"), P("grp", "col")),
        out_specs=(P(("grp", "row"), "col"), P(("row", "col"), "grp"), P(("row", "col"), "grp")),
        check_vma=False,
    )
```

```python
import functools

import jax
import jax.numpy as jnp
from jax import lax
from jax.experimental import pallas as pl
from jax.experimental.pallas import tpu as pltpu
from jax.sharding import PartitionSpec as P

SHRINK = 2.0 ** -16
BF16 = jnp.bfloat16
F32 = jnp.float32
CONTRACT = (((0,), (0,)), ((), ()))


def gather_kernel(
    rows_ref, t_hbm, c_hbm, a_hbm, g_hbm,
    u_out, v_out, xl_out, xs_out, yl_out, ys_out,
    t_v, c_v, a_v, g_v, oh_v, px_v, q_v, r1_s, r1_r, r2_s, r2_r,
    w_s, w_r, w_v, h_s, h_r, u_v, v_v, xl_v, xs_v, yl_v, ys_v, xlt_v, ylt_v,
    load_sem, out_sem, send_sem, recv_sem,
):
    grp, z, c = lax.axis_index("grp"), lax.axis_index("row"), lax.axis_index("col")
    x, k = grp // 2, grp % 2
    oc, ok, ox = 1 - c, 1 - k, 1 - x
    z1 = z + 1 - 2 * (z % 2)
    z2 = (z + 2) % 4
    z3 = (z1 + 2) % 4
    places = (z, z2, z1, z3)
    to_y = {"col": oc}
    to_k = {"grp": 2 * x + ok}
    to_x = {"grp": 2 * ox + k}
    to_xk = {"grp": 2 * ox + ok}
    to_z1 = {"row": z1}
    to_z2 = {"row": z2}
    tok = t_v.shape[0]
    share = g_v.shape[1]
    half = xl_v.shape[2]
    out_rows = u_v.shape[1]
    phases = ((c, 0, tok), (oc, 0, tok // 2), (oc, tok // 2, tok // 2))

    names = {}
    sends = []

    def copy(name, src, dst, where):
        i = names.setdefault(name, len(names))
        return pltpu.make_async_remote_copy(
            src_ref=src, dst_ref=dst, send_sem=send_sem.at[i], recv_sem=recv_sem.at[i],
            device_id=where, device_id_type=pl.DeviceIdType.MESH,
        )

    def send(name, src, dst, where):
        out = copy(name, src, dst, where)
        out.start()
        sends.append(out)

    def await_in(name, dst, where):
        copy(name, dst, dst, where).wait_recv()

    def load_a(block, sem):
        rows = pl.ds(pl.multiple_of(block * out_rows, out_rows), out_rows)
        return pltpu.make_async_copy(a_hbm.at[rows], a_v.at[rows], load_sem.at[sem])

    odd = z % 2
    away_blocks = (1 - odd, 3 - odd)
    home_blocks = (odd, 2 + odd)
    loads = [
        pltpu.make_async_copy(t_hbm, t_v, load_sem.at[2]),
        load_a(away_blocks[0], 3),
        load_a(away_blocks[1], 4),
        pltpu.make_async_copy(c_hbm, c_v.at[c], load_sem.at[0]),
        pltpu.make_async_copy(
            g_hbm.at[:, pl.ds(pl.multiple_of(z * share, 128), share)], g_v, load_sem.at[1]
        ),
        load_a(home_blocks[0], 5),
        load_a(home_blocks[1], 6),
    ]
    for load in loads:
        load.start()

    barrier = pltpu.get_barrier_semaphore()
    partners = [to_y, to_k, to_x, to_xk, to_z1, to_z2]
    for where in partners:
        pl.semaphore_signal(barrier, inc=1, device_id=where, device_id_type=pl.DeviceIdType.MESH)
    pl.semaphore_wait(barrier, len(partners))

    for ph in (1, 2):
        part = pl.ds(phases[ph][1], phases[ph][2])
        send(("cot", ph), c_hbm.at[part], c_v.at[c, part], to_y)

    hot = lax.broadcasted_iota(jnp.int32, (tok, rows_ref.shape[1]), 0) + c * tok == rows_ref[...]
    oh_v[c] = jnp.where(hot, 1.0, 0.0).astype(BF16)
    send("hot", oh_v.at[c], oh_v.at[c], to_y)

    def pick(block, values):
        return lax.dot_general(oh_v[block], values, CONTRACT, preferred_element_type=F32).astype(BF16)

    def v_at(ph, core, side, step):
        block, first, count = phases[ph]
        row = pl.multiple_of(block * tok + first + (2 * core + side) * (count // 4), count // 4)
        return v_v.at[
            pl.ds(row, count // 4), pl.ds(pl.multiple_of(places[step] * share, 128), share)
        ]

    def cut(ph):
        return pl.ds(0, phases[ph][2] // 4)

    def product(ph):
        block, first, count = phases[ph]
        q = jnp.dot(c_v[block, first:first + count], g_v[...], preferred_element_type=F32)
        q_v[ph, :, cut(ph)] = q.reshape(4, count // 4, share)
        r1_s[ph, :, cut(ph)] = q_v[ph, pl.ds(2 * ok, 2), cut(ph)].astype(BF16)
        send(("r1", ph), r1_s.at[ph, :, cut(ph)], r1_r.at[ph, :, cut(ph)], to_k)

    def across(ph):
        await_in(("r1", ph), r1_r.at[ph, :, cut(ph)], to_k)
        r2_s[ph, cut(ph)] = (
            q_v[ph, 2 * k + ox, cut(ph)] + r1_r[ph, ox, cut(ph)].astype(F32)
        ).astype(BF16)
        send(("r2", ph), r2_s.at[ph, cut(ph)], r2_r.at[ph, cut(ph)], to_x)

    def finish(ph):
        await_in(("r2", ph), r2_r.at[ph, cut(ph)], to_x)
        total = (
            q_v[ph, 2 * k + x, cut(ph)] + r1_r[ph, x, cut(ph)].astype(F32)
            + r2_r[ph, cut(ph)].astype(F32)
        )
        mine = v_at(ph, k, x, 0)
        mine[...] = total.astype(BF16)
        send(("v", ph, 1), mine, mine, to_z2)
        send(("v", ph, 2), mine, mine, to_z1)
        send(("vx", ph, 0), mine, mine, to_x)
        send(("vk", ph, 0), mine, mine, to_k)

    def spread(ph, step):
        got = v_at(ph, k, x, step)
        await_in(("v", ph, step), got, to_z1)
        if step == 1:
            send(("v", ph, 3), got, got, to_z1)
        send(("vx", ph, step), got, got, to_x)
        send(("vk", ph, step), got, got, to_k)

    def relay(ph, step):
        got = v_at(ph, k, ox, step)
        await_in(("vx", ph, step), got, to_x)
        send(("vk", ph, 4 + step), got, got, to_k)

    def collect(ph):
        for step in range(4):
            await_in(("vk", ph, step), v_at(ph, ok, x, step), to_k)
        for step in range(4):
            await_in(("vk", ph, 4 + step), v_at(ph, ok, ox, step), to_k)

    def u_part(block):
        rows = a_v[pl.ds(pl.multiple_of(block * out_rows, out_rows), out_rows), :]
        return lax.dot_general(t_v[...], rows, (((1,), (1,)), ((), ())), preferred_element_type=F32)

    def at_half(ref, index):
        return ref.at[:, pl.ds(pl.multiple_of(index * half, 128), half)]

    def await_cot(ph):
        part = pl.ds(phases[ph][1], phases[ph][2])
        await_in(("cot", ph), c_v.at[oc, part], to_y)

    has_span = grp == z
    is_z2 = grp == z2
    is_z1 = grp == z1
    span = xs_v.at[c]
    x_z2 = copy("x2", span, span, to_z2)
    x_z1 = copy("x1", span, span, to_z1)

    loads[0].wait()
    px_v[...] = pick(c, t_v[...])

    @pl.when(has_span)
    def _():
        xs_v[c] = px_v[...]
        x_z2.start()
        x_z1.start()

    t_v[...] = t_v[...] * jnp.asarray(SHRINK, BF16)
    for i in range(2):
        loads[1 + i].wait()
        w_s[i] = u_part(away_blocks[i]).astype(BF16)
    send("w", w_s, w_r, to_z1)
    loads[3].wait()
    loads[4].wait()
    product(0)
    ys_v[c] = pick(c, c_v[c])

    def y_copies(block):
        left = ys_v.at[block, :, pl.ds(pl.multiple_of(c * half, 128), half)]
        own = 0 if block is c else 1
        return left, [
            copy(("yl", own, i), left, yl_v.at[block], w) for i, w in enumerate([to_k, to_x, to_xk])
        ]

    left_c, y_c = y_copies(c)
    left_oc, y_oc = y_copies(oc)

    @pl.when(has_span)
    def _():
        for out in y_c:
            out.start()
        yl_v[c] = left_c[...]

    across(0)
    for i in range(2):
        loads[5 + i].wait()
        w_v[i] = u_part(home_blocks[i])
    finish(0)
    await_cot(1)
    product(1)

    @pl.when(is_z2)
    def _():
        x_z2.wait_recv()
        x_z1.start()

    across(1)
    await_in("w", w_r, to_z1)
    mine, away = z // 2, 1 - z // 2
    h_s[...] = (w_v[away] + w_r[away].astype(F32)).astype(BF16)
    send("h", h_s, h_r, to_z2)
    spread(0, 1)
    finish(1)
    spread(0, 2)
    await_cot(2)
    product(2)
    spread(0, 3)
    across(2)
    send("xl", at_half(px_v, oc), xl_v.at[c], to_y)
    xl_v[c] = at_half(px_v, c)[...]
    spread(1, 1)
    spread(1, 2)

    @pl.when(jnp.logical_or(is_z1, grp == z3))
    def _():
        x_z1.wait_recv()

    send("xy", span, span, to_y)
    finish(2)
    await_in("hot", oh_v.at[oc], to_y)
    ys_v[oc] = pick(oc, c_v[oc])

    @pl.when(has_span)
    def _():
        for out in y_oc:
            out.start()
        yl_v[oc] = left_oc[...]

    for step in range(4):
        relay(0, step)
    spread(1, 3)
    await_in("h", h_r, to_z2)
    u = w_v[mine] + w_r[mine].astype(F32) + h_r[...].astype(F32)
    u_v[c] = u.T.astype(BF16)
    send("u", u_v.at[c], u_v.at[c], to_y)
    for step in range(3):
        relay(1, step)
    for step in range(1, 4):
        spread(2, step)
    relay(1, 3)
    for step in range(4):
        relay(2, step)
    collect(0)

    outs = []

    def put(src, dst):
        out = pltpu.make_async_copy(src, dst, out_sem.at[len(outs)])
        out.start()
        outs.append(out)

    def put_v(ph):
        block, first, count = phases[ph]
        rows = pl.ds(pl.multiple_of(block * tok + first, count), count)
        put(v_v.at[rows], v_out.at[rows])

    put_v(0)
    put(ys_v, ys_out)
    collect(1)
    put_v(1)
    await_in("xl", xl_v.at[oc], to_y)
    xlt_v[...] = xl_v[...].reshape(xlt_v.shape[::-1]).T
    put(xlt_v, xl_out)

    @pl.when(grp == 2 * (z // 2) + (1 - z % 2))
    def _():
        y_c[0].wait_recv()
        y_oc[0].wait_recv()

    @pl.when(grp == 2 * (1 - z // 2) + z % 2)
    def _():
        y_c[1].wait_recv()
        y_oc[1].wait_recv()

    @pl.when(grp == 2 * (1 - z // 2) + (1 - z % 2))
    def _():
        y_c[2].wait_recv()
        y_oc[2].wait_recv()

    ylt_v[...] = yl_v[...].reshape(ylt_v.shape[::-1]).T
    put(ylt_v, yl_out)
    await_in("xy", xs_v.at[oc], to_y)
    put(xs_v, xs_out)
    await_in("u", u_v.at[oc], to_y)
    for block in range(2):
        put(u_v.at[block], u_out.at[:, block * tok:(block + 1) * tok])
    collect(2)
    put_v(2)

    @pl.when(has_span)
    def _():
        x_z2.wait_send()
        x_z1.wait_send()
        for out in y_c + y_oc:
            out.wait_send()

    @pl.when(is_z2)
    def _():
        x_z1.wait_send()

    for out in sends:
        out.wait_send()
    for out in outs:
        out.wait()


def gather(rows, tokens_in, cotangent, act_inverse, grad_inverse, n_row):
    tok, feat = tokens_in.shape
    samples = rows.shape[1]
    share = grad_inverse.shape[1] // n_row
    out_rows = feat // n_row
    half = feat // 2
    piece = tok // 4
    v_shape, span = (2 * tok, grad_inverse.shape[1]), (2, samples, feat)
    left, left_t = (2, samples, half), (half, 2 * samples)
    shapes = [(out_rows, 2 * tok), v_shape, left_t, span, left_t, span]
    held = [(2, out_rows, tok), v_shape, left, span, left, span, left_t, left_t]
    vmem = pltpu.VMEM
    return pl.pallas_call(
        gather_kernel,
        out_shape=[jax.ShapeDtypeStruct(s, BF16) for s in shapes],
        in_specs=[pl.BlockSpec(memory_space=vmem)] + [pl.BlockSpec(memory_space=pl.ANY)] * 4,
        out_specs=[pl.BlockSpec(memory_space=pl.ANY)] * 6,
        scratch_shapes=[
            vmem((tok, feat), BF16),
            vmem((2, tok, feat), BF16),
            vmem(act_inverse.shape, BF16),
            vmem((feat, share), BF16),
            vmem((2, tok, samples), BF16),
            vmem((samples, feat), BF16),
            vmem((3, 4, piece, share), F32),
            vmem((3, 2, piece, share), BF16),
            vmem((3, 2, piece, share), BF16),
            vmem((3, piece, share), BF16),
            vmem((3, piece, share), BF16),
            vmem((2, tok, out_rows), BF16),
            vmem((2, tok, out_rows), BF16),
            vmem((2, tok, out_rows), F32),
            vmem((tok, out_rows), BF16),
            vmem((tok, out_rows), BF16),
        ] + [vmem(s, BF16) for s in held] + [
            pltpu.SemaphoreType.DMA((7,)),
            pltpu.SemaphoreType.DMA((9,)),
            pltpu.SemaphoreType.DMA((72,)),
            pltpu.SemaphoreType.DMA((72,)),
        ],
        compiler_params=pltpu.CompilerParams(
            collective_id=0, has_side_effects=True, vmem_limit_bytes=60 * 2 ** 20
        ),
        cost_estimate=pl.CostEstimate(flops=3 * 10 ** 9, bytes_accessed=10 ** 7, transcendentals=0),
    )(rows, tokens_in, cotangent, act_inverse, grad_inverse)


def product_kernel(total, ut, v, xt, xs, yt, ys, p_out, a_out, g_out):
    a_out[...] = jnp.dot(xt[...], xs[...], preferred_element_type=F32) * (1 / total)
    g_out[...] = jnp.dot(yt[...], ys[...], preferred_element_type=F32) * (1 / total)
    p_out[...] = jnp.dot(ut[...], v[...], preferred_element_type=F32) * (1 / SHRINK)


def products(ut, v, xt, xs, yt, ys):
    steps = 6
    total = xt.shape[1]

    def whole(a):
        return pl.BlockSpec(a.shape, lambda i: (0, 0))

    def cut(rows, width):
        return pl.BlockSpec((rows, width // steps), lambda i: (0, i))

    return pl.pallas_call(
        functools.partial(product_kernel, total),
        grid=(steps,),
        in_specs=[
            whole(ut), cut(v.shape[0], v.shape[1]),
            whole(xt), cut(total, xs.shape[1]), whole(yt), cut(total, ys.shape[1]),
        ],
        out_specs=[
            cut(ut.shape[0], v.shape[1]), cut(xt.shape[0], xs.shape[1]), cut(yt.shape[0], ys.shape[1])
        ],
        out_shape=[
            jax.ShapeDtypeStruct((ut.shape[0], v.shape[1]), F32),
            jax.ShapeDtypeStruct((xt.shape[0], xs.shape[1]), F32),
            jax.ShapeDtypeStruct((yt.shape[0], ys.shape[1]), F32),
        ],
        compiler_params=pltpu.CompilerParams(vmem_limit_bytes=60 * 2 ** 20),
        cost_estimate=pl.CostEstimate(flops=10 ** 9, bytes_accessed=17 * 10 ** 6, transcendentals=0),
    )(ut, v, xt, xs, yt, ys)


def flat(a):
    return a.reshape(-1, a.shape[-1])


def body_kernels(tokens_in, cotangent, sample_rows, act_inverse, grad_inverse):
    ut, v, xt, xs, yt, ys = gather(
        sample_rows[None], tokens_in, cotangent, act_inverse, grad_inverse, lax.axis_size("row")
    )
    return tuple(products(ut, v, xt, flat(xs), yt, flat(ys)))


def body(tokens_in, cotangent, sample_rows, act_inverse, grad_inverse):
    feat_row = tokens_in.shape[1]
    feat_grp = cotangent.shape[1]
    n_row = lax.axis_size("row")
    n_col = lax.axis_size("col")
    n_grp = lax.axis_size("grp")
    width = feat_row * n_row
    contract = (((0,), (0,)), ((), ()))
    col_index = lax.axis_index("col")
    grp_index = lax.axis_index("grp")
    row_index = lax.axis_index("row")
    small = tokens_in * jnp.asarray(SHRINK, tokens_in.dtype)
    part_u = lax.dot_general(
        small, act_inverse, (((1,), (1,)), ((), ())), preferred_element_type=jnp.float32
    )
    u = lax.psum_scatter(part_u.astype(jnp.bfloat16), "row", scatter_dimension=1, tiled=True)
    u = lax.all_gather(u, "col", axis=0, tiled=True)
    all_cot = lax.all_gather(cotangent, "col", axis=0, tiled=True)
    share = grad_inverse.shape[1] // n_row
    mine = lax.dynamic_slice_in_dim(grad_inverse, row_index * share, share, 1)
    part_v = jnp.dot(all_cot, mine, preferred_element_type=jnp.float32)
    v = lax.psum(part_v.astype(jnp.bfloat16), "grp")
    v = lax.all_gather(v, "row", axis=1, tiled=True)
    precond = lax.dot_general(u, v, contract, preferred_element_type=jnp.float32) * (1 / SHRINK)
    offsets = sample_rows - col_index * tokens_in.shape[0]
    picked_x = jnp.take(tokens_in, offsets, axis=0)
    picked_g = jnp.take(cotangent, offsets, axis=0)
    samples = picked_x.shape[0]
    total = samples * n_col
    act_panel = lax.all_gather(picked_x[None], ("row", "col"), axis=0, tiled=True).reshape(
        n_row, total, feat_row
    )
    grad_panel = lax.all_gather(picked_g[None], ("grp", "col"), axis=0, tiled=True).reshape(
        n_grp, total, feat_grp
    )
    tile = width // (n_row * n_col)
    first = (row_index * n_col + col_index) * tile
    act_left = lax.dynamic_slice(
        act_panel, (first // feat_row, 0, first % feat_row), (1, total, tile)
    )[0]
    per = feat_grp // feat_row
    act_span = lax.dynamic_slice_in_dim(act_panel, grp_index * per, per, 0)
    act_cov = jnp.einsum("sa,psf->apf", act_left, act_span, preferred_element_type=jnp.float32)
    act_cov = act_cov.reshape(tile, feat_grp) / total
    grad_left = lax.dynamic_slice(
        grad_panel, (first // feat_grp, 0, first % feat_grp), (1, total, tile)
    )[0]
    grad_span = lax.dynamic_index_in_dim(grad_panel, grp_index, 0, keepdims=False)
    grad_cov = (
        lax.dot_general(grad_left, grad_span, contract, preferred_element_type=jnp.float32) / total
    )
    return (precond, act_cov, grad_cov)


def solution(mesh):
    sizes = tuple(mesh.shape[name] for name in ("grp", "row", "col"))
    return jax.shard_map(
        body_kernels if sizes == (4, 4, 2) else body,
        mesh=mesh,
        in_specs=(P("col", "row"), P("col", "grp"), P("col"), P("grp", "row"), P("grp", "col")),
        out_specs=(P(("grp", "row"), "col"), P(("row", "col"), "grp"), P(("row", "col"), "grp")),
        check_vma=False,
    )
```

```python
import functools

import jax
import jax.numpy as jnp
from jax import lax
from jax.experimental import pallas as pl
from jax.experimental.pallas import tpu as pltpu
from jax.sharding import PartitionSpec as P

SHRINK = 2.0 ** -16
BF16 = jnp.bfloat16
F32 = jnp.float32
CONTRACT = (((0,), (0,)), ((), ()))


def gather_kernel(
    rows_ref, t_hbm, c_hbm, a_hbm, g_hbm,
    u_out, v_out, xl_out, xs_out, yl_out, ys_out,
    t_v, c_v, a_v, g_v, oh_v, px_v, q_v, r1_s, r1_r, r2_s, r2_r,
    qb_v, b1_s, b1_r, b2_s, b2_r,
    w_s, w_r, w_v, h_s, h_r, u_v, v_v, xl_v, xs_v, yl_v, ys_v, xlt_v, ylt_v,
    load_sem, out_sem, send_sem, recv_sem,
):
    grp, z, c = lax.axis_index("grp"), lax.axis_index("row"), lax.axis_index("col")
    x, k = grp // 2, grp % 2
    oc, ok, ox = 1 - c, 1 - k, 1 - x
    z1 = z + 1 - 2 * (z % 2)
    z2 = (z + 2) % 4
    z3 = (z1 + 2) % 4
    places = (z, z2, z1, z3)
    to_y = {"col": oc}
    to_k = {"grp": 2 * x + ok}
    to_x = {"grp": 2 * ox + k}
    to_xk = {"grp": 2 * ox + ok}
    to_z1 = {"row": z1}
    to_z2 = {"row": z2}
    tok = t_v.shape[0]
    share = g_v.shape[2]
    half = xl_v.shape[2]
    out_rows = u_v.shape[1]
    phases = ((c, 0, tok), (oc, 0, tok // 2), (oc, tok // 2, tok // 2))

    names = {}
    sends = []

    def copy(name, src, dst, where):
        i = names.setdefault(name, len(names))
        return pltpu.make_async_remote_copy(
            src_ref=src, dst_ref=dst, send_sem=send_sem.at[i], recv_sem=recv_sem.at[i],
            device_id=where, device_id_type=pl.DeviceIdType.MESH,
        )

    def send(name, src, dst, where):
        out = copy(name, src, dst, where)
        out.start()
        sends.append(out)

    def await_in(name, dst, where):
        copy(name, dst, dst, where).wait_recv()

    def load_a(block, sem):
        rows = pl.ds(pl.multiple_of(block * out_rows, out_rows), out_rows)
        return pltpu.make_async_copy(a_hbm.at[rows], a_v.at[rows], load_sem.at[sem])

    def load_g(part, sem):
        columns = pl.ds(pl.multiple_of(part * share, 128), share)
        return pltpu.make_async_copy(g_hbm.at[:, columns], g_v.at[part], load_sem.at[sem])

    odd = z % 2
    away_blocks = (1 - odd, 3 - odd)
    home_blocks = (odd, 2 + odd)
    loads = [
        pltpu.make_async_copy(t_hbm, t_v, load_sem.at[2]),
        load_a(away_blocks[0], 3),
        load_a(away_blocks[1], 4),
        pltpu.make_async_copy(c_hbm, c_v.at[c], load_sem.at[0]),
        load_g(z, 1),
        load_a(home_blocks[0], 5),
        load_a(home_blocks[1], 6),
    ] + [load_g((z + i) % 4, 6 + i) for i in range(1, 4)]
    for load in loads:
        load.start()

    barrier = pltpu.get_barrier_semaphore()
    partners = [to_y, to_k, to_x, to_xk, to_z1, to_z2]
    for where in partners:
        pl.semaphore_signal(barrier, inc=1, device_id=where, device_id_type=pl.DeviceIdType.MESH)
    pl.semaphore_wait(barrier, len(partners))

    for ph in (1, 2):
        part = pl.ds(phases[ph][1], phases[ph][2])
        send(("cot", ph), c_hbm.at[part], c_v.at[c, part], to_y)

    hot = lax.broadcasted_iota(jnp.int32, (tok, rows_ref.shape[1]), 0) + c * tok == rows_ref[...]
    oh_v[c] = jnp.where(hot, 1.0, 0.0).astype(BF16)
    send("hot", oh_v.at[c], oh_v.at[c], to_y)

    def pick(block, values):
        return lax.dot_general(oh_v[block], values, CONTRACT, preferred_element_type=F32).astype(BF16)

    def v_at(ph, core, side, step):
        block, first, count = phases[ph]
        row = pl.multiple_of(block * tok + first + (2 * core + side) * (count // 4), count // 4)
        return v_v.at[
            pl.ds(row, count // 4), pl.ds(pl.multiple_of(places[step] * share, 128), share)
        ]

    def cut(ph):
        return pl.ds(0, phases[ph][2] // 4)

    def product(ph):
        block, first, count = phases[ph]
        q = jnp.dot(c_v[block, first:first + count], g_v[z], preferred_element_type=F32)
        q_v[ph, :, cut(ph)] = q.reshape(4, count // 4, share)
        r1_s[ph, :, cut(ph)] = q_v[ph, pl.ds(2 * ok, 2), cut(ph)].astype(BF16)
        send(("r1", ph), r1_s.at[ph, :, cut(ph)], r1_r.at[ph, :, cut(ph)], to_k)

    def across(ph):
        await_in(("r1", ph), r1_r.at[ph, :, cut(ph)], to_k)
        r2_s[ph, cut(ph)] = (
            q_v[ph, 2 * k + ox, cut(ph)] + r1_r[ph, ox, cut(ph)].astype(F32)
        ).astype(BF16)
        send(("r2", ph), r2_s.at[ph, cut(ph)], r2_r.at[ph, cut(ph)], to_x)

    def finish(ph):
        await_in(("r2", ph), r2_r.at[ph, cut(ph)], to_x)
        total = (
            q_v[ph, 2 * k + x, cut(ph)] + r1_r[ph, x, cut(ph)].astype(F32)
            + r2_r[ph, cut(ph)].astype(F32)
        )
        mine = v_at(ph, k, x, 0)
        mine[...] = total.astype(BF16)
        send(("v", ph, 1), mine, mine, to_z2)
        send(("v", ph, 2), mine, mine, to_z1)
        send(("vx", ph, 0), mine, mine, to_x)
        send(("vk", ph, 0), mine, mine, to_k)

    def spread(ph, step):
        got = v_at(ph, k, x, step)
        await_in(("v", ph, step), got, to_z1)
        if step == 1:
            send(("v", ph, 3), got, got, to_z1)
        send(("vx", ph, step), got, got, to_x)
        send(("vk", ph, step), got, got, to_k)

    def relay(ph, step):
        got = v_at(ph, k, ox, step)
        await_in(("vx", ph, step), got, to_x)
        send(("vk", ph, 4 + step), got, got, to_k)

    def collect(ph):
        for step in range(4):
            await_in(("vk", ph, step), v_at(ph, ok, x, step), to_k)
        for step in range(4):
            await_in(("vk", ph, 4 + step), v_at(ph, ok, ox, step), to_k)

    def rows_b(ph, core):
        block, first, count = phases[ph]
        return pl.ds(pl.multiple_of(block * tok + first + core * (count // 2), count // 2), count // 2)

    def product_b(ph, j):
        block, first, count = phases[ph]
        unit = 4 * (ph - 1) + j
        q = jnp.dot(c_v[block, first:first + count], g_v[j], preferred_element_type=F32)
        qb_v[unit] = q.reshape(2, count // 2, share)
        b1_s[unit] = qb_v[unit, ok].astype(BF16)
        send(("b1", unit), b1_s.at[unit], b1_r.at[unit], to_k)

    def across_b(ph, j):
        unit = 4 * (ph - 1) + j
        await_in(("b1", unit), b1_r.at[unit], to_k)
        total = qb_v[unit, k] + b1_r[unit].astype(F32)
        qb_v[unit, k] = total
        b2_s[unit] = total.astype(BF16)
        send(("b2", unit), b2_s.at[unit], b2_r.at[unit], to_x)

    def finish_b(ph, j):
        unit = 4 * (ph - 1) + j
        await_in(("b2", unit), b2_r.at[unit], to_x)
        mine = v_v.at[rows_b(ph, k), j * share:(j + 1) * share]
        mine[...] = (qb_v[unit, k] + b2_r[unit].astype(F32)).astype(BF16)
        send(("bk", unit), mine, mine, to_k)

    def collect_b(ph):
        for j in range(4):
            got = v_v.at[rows_b(ph, ok), j * share:(j + 1) * share]
            await_in(("bk", 4 * (ph - 1) + j), got, to_k)

    def run_b(ph):
        product_b(ph, 0)
        for j in range(1, 4):
            product_b(ph, j)
            across_b(ph, j - 1)
        across_b(ph, 3)

    def u_part(block):
        rows = a_v[pl.ds(pl.multiple_of(block * out_rows, out_rows), out_rows), :]
        return lax.dot_general(t_v[...], rows, (((1,), (1,)), ((), ())), preferred_element_type=F32)

    def at_half(ref, index):
        return ref.at[:, pl.ds(pl.multiple_of(index * half, 128), half)]

    def await_cot(ph):
        part = pl.ds(phases[ph][1], phases[ph][2])
        await_in(("cot", ph), c_v.at[oc, part], to_y)

    has_span = grp == z
    is_z2 = grp == z2
    is_z1 = grp == z1
    span = xs_v.at[c]
    x_z2 = copy("x2", span, span, to_z2)
    x_z1 = copy("x1", span, span, to_z1)

    loads[0].wait()
    px_v[...] = pick(c, t_v[...])

    @pl.when(has_span)
    def _():
        xs_v[c] = px_v[...]
        x_z2.start()
        x_z1.start()

    t_v[...] = t_v[...] * jnp.asarray(SHRINK, BF16)
    for i in range(2):
        loads[1 + i].wait()
        w_s[i] = u_part(away_blocks[i]).astype(BF16)
    send("w", w_s, w_r, to_z1)
    loads[3].wait()
    loads[4].wait()
    product(0)
    ys_v[c] = pick(c, c_v[c])

    def y_copies(block):
        left = ys_v.at[block, :, pl.ds(pl.multiple_of(c * half, 128), half)]
        own = 0 if block is c else 1
        return left, [
            copy(("yl", own, i), left, yl_v.at[block], w) for i, w in enumerate([to_k, to_x, to_xk])
        ]

    left_c, y_c = y_copies(c)
    left_oc, y_oc = y_copies(oc)

    @pl.when(has_span)
    def _():
        for out in y_c:
            out.start()
        yl_v[c] = left_c[...]

    across(0)
    for i in range(2):
        loads[5 + i].wait()
        w_v[i] = u_part(home_blocks[i])
    finish(0)
    await_cot(1)
    for i in range(7, 10):
        loads[i].wait()
    run_b(1)

    @pl.when(is_z2)
    def _():
        x_z2.wait_recv()
        x_z1.start()

    await_in("w", w_r, to_z1)
    mine, away = z // 2, 1 - z // 2
    h_s[...] = (w_v[away] + w_r[away].astype(F32)).astype(BF16)
    send("h", h_s, h_r, to_z2)
    spread(0, 1)
    spread(0, 2)
    await_cot(2)
    run_b(2)
    spread(0, 3)
    for j in range(4):
        finish_b(1, j)
    send("xl", at_half(px_v, oc), xl_v.at[c], to_y)
    xl_v[c] = at_half(px_v, c)[...]

    @pl.when(jnp.logical_or(is_z1, grp == z3))
    def _():
        x_z1.wait_recv()

    send("xy", span, span, to_y)
    await_in("hot", oh_v.at[oc], to_y)
    ys_v[oc] = pick(oc, c_v[oc])

    @pl.when(has_span)
    def _():
        for out in y_oc:
            out.start()
        yl_v[oc] = left_oc[...]

    await_in("h", h_r, to_z2)
    u = w_v[mine] + w_r[mine].astype(F32) + h_r[...].astype(F32)
    u_v[c] = u.T.astype(BF16)
    send("u", u_v.at[c], u_v.at[c], to_y)
    for step in range(4):
        relay(0, step)
    for j in range(4):
        finish_b(2, j)
    collect(0)

    outs = []

    def put(src, dst):
        out = pltpu.make_async_copy(src, dst, out_sem.at[len(outs)])
        out.start()
        outs.append(out)

    def put_v(ph):
        block, first, count = phases[ph]
        rows = pl.ds(pl.multiple_of(block * tok + first, count), count)
        put(v_v.at[rows], v_out.at[rows])

    put_v(0)
    put(ys_v, ys_out)
    collect_b(1)
    put_v(1)
    await_in("xl", xl_v.at[oc], to_y)
    xlt_v[...] = xl_v[...].reshape(xlt_v.shape[::-1]).T
    put(xlt_v, xl_out)

    @pl.when(grp == 2 * (z // 2) + (1 - z % 2))
    def _():
        y_c[0].wait_recv()
        y_oc[0].wait_recv()

    @pl.when(grp == 2 * (1 - z // 2) + z % 2)
    def _():
        y_c[1].wait_recv()
        y_oc[1].wait_recv()

    @pl.when(grp == 2 * (1 - z // 2) + (1 - z % 2))
    def _():
        y_c[2].wait_recv()
        y_oc[2].wait_recv()

    ylt_v[...] = yl_v[...].reshape(ylt_v.shape[::-1]).T
    put(ylt_v, yl_out)
    await_in("xy", xs_v.at[oc], to_y)
    put(xs_v, xs_out)
    await_in("u", u_v.at[oc], to_y)
    for block in range(2):
        put(u_v.at[block], u_out.at[:, block * tok:(block + 1) * tok])
    collect_b(2)
    put_v(2)

    @pl.when(has_span)
    def _():
        x_z2.wait_send()
        x_z1.wait_send()
        for out in y_c + y_oc:
            out.wait_send()

    @pl.when(is_z2)
    def _():
        x_z1.wait_send()

    for out in sends:
        out.wait_send()
    for out in outs:
        out.wait()


def gather(rows, tokens_in, cotangent, act_inverse, grad_inverse, n_row):
    tok, feat = tokens_in.shape
    samples = rows.shape[1]
    share = grad_inverse.shape[1] // n_row
    out_rows = feat // n_row
    half = feat // 2
    piece = tok // 4
    v_shape, span = (2 * tok, grad_inverse.shape[1]), (2, samples, feat)
    left, left_t = (2, samples, half), (half, 2 * samples)
    shapes = [(out_rows, 2 * tok), v_shape, left_t, span, left_t, span]
    held = [(2, out_rows, tok), v_shape, left, span, left, span, left_t, left_t]
    vmem = pltpu.VMEM
    return pl.pallas_call(
        gather_kernel,
        out_shape=[jax.ShapeDtypeStruct(s, BF16) for s in shapes],
        in_specs=[pl.BlockSpec(memory_space=vmem)] + [pl.BlockSpec(memory_space=pl.ANY)] * 4,
        out_specs=[pl.BlockSpec(memory_space=pl.ANY)] * 6,
        scratch_shapes=[
            vmem((tok, feat), BF16),
            vmem((2, tok, feat), BF16),
            vmem(act_inverse.shape, BF16),
            vmem((n_row, feat, share), BF16),
            vmem((2, tok, samples), BF16),
            vmem((samples, feat), BF16),
            vmem((1, 4, piece, share), F32),
            vmem((1, 2, piece, share), BF16),
            vmem((1, 2, piece, share), BF16),
            vmem((1, piece, share), BF16),
            vmem((1, piece, share), BF16),
            vmem((8, 2, piece, share), F32),
            vmem((8, piece, share), BF16),
            vmem((8, piece, share), BF16),
            vmem((8, piece, share), BF16),
            vmem((8, piece, share), BF16),
            vmem((2, tok, out_rows), BF16),
            vmem((2, tok, out_rows), BF16),
            vmem((2, tok, out_rows), F32),
            vmem((tok, out_rows), BF16),
            vmem((tok, out_rows), BF16),
        ] + [vmem(s, BF16) for s in held] + [
            pltpu.SemaphoreType.DMA((10,)),
            pltpu.SemaphoreType.DMA((9,)),
            pltpu.SemaphoreType.DMA((72,)),
            pltpu.SemaphoreType.DMA((72,)),
        ],
        compiler_params=pltpu.CompilerParams(
            collective_id=0, has_side_effects=True, vmem_limit_bytes=60 * 2 ** 20
        ),
        cost_estimate=pl.CostEstimate(flops=3 * 10 ** 9, bytes_accessed=10 ** 7, transcendentals=0),
    )(rows, tokens_in, cotangent, act_inverse, grad_inverse)


def product_kernel(total, ut, v, xt, xs, yt, ys, p_out, a_out, g_out):
    a_out[...] = jnp.dot(xt[...], xs[...], preferred_element_type=F32) * (1 / total)
    g_out[...] = jnp.dot(yt[...], ys[...], preferred_element_type=F32) * (1 / total)
    p_out[...] = jnp.dot(ut[...], v[...], preferred_element_type=F32) * (1 / SHRINK)


def products(ut, v, xt, xs, yt, ys):
    steps = 6
    total = xt.shape[1]

    def whole(a):
        return pl.BlockSpec(a.shape, lambda i: (0, 0))

    def cut(rows, width):
        return pl.BlockSpec((rows, width // steps), lambda i: (0, i))

    return pl.pallas_call(
        functools.partial(product_kernel, total),
        grid=(steps,),
        in_specs=[
            whole(ut), cut(v.shape[0], v.shape[1]),
            whole(xt), cut(total, xs.shape[1]), whole(yt), cut(total, ys.shape[1]),
        ],
        out_specs=[
            cut(ut.shape[0], v.shape[1]), cut(xt.shape[0], xs.shape[1]), cut(yt.shape[0], ys.shape[1])
        ],
        out_shape=[
            jax.ShapeDtypeStruct((ut.shape[0], v.shape[1]), F32),
            jax.ShapeDtypeStruct((xt.shape[0], xs.shape[1]), F32),
            jax.ShapeDtypeStruct((yt.shape[0], ys.shape[1]), F32),
        ],
        compiler_params=pltpu.CompilerParams(vmem_limit_bytes=60 * 2 ** 20),
        cost_estimate=pl.CostEstimate(flops=10 ** 9, bytes_accessed=17 * 10 ** 6, transcendentals=0),
    )(ut, v, xt, xs, yt, ys)


def flat(a):
    return a.reshape(-1, a.shape[-1])


def body_kernels(tokens_in, cotangent, sample_rows, act_inverse, grad_inverse):
    ut, v, xt, xs, yt, ys = gather(
        sample_rows[None], tokens_in, cotangent, act_inverse, grad_inverse, lax.axis_size("row")
    )
    return tuple(products(ut, v, xt, flat(xs), yt, flat(ys)))


def body(tokens_in, cotangent, sample_rows, act_inverse, grad_inverse):
    feat_row = tokens_in.shape[1]
    feat_grp = cotangent.shape[1]
    n_row = lax.axis_size("row")
    n_col = lax.axis_size("col")
    n_grp = lax.axis_size("grp")
    width = feat_row * n_row
    contract = (((0,), (0,)), ((), ()))
    col_index = lax.axis_index("col")
    grp_index = lax.axis_index("grp")
    row_index = lax.axis_index("row")
    small = tokens_in * jnp.asarray(SHRINK, tokens_in.dtype)
    part_u = lax.dot_general(
        small, act_inverse, (((1,), (1,)), ((), ())), preferred_element_type=jnp.float32
    )
    u = lax.psum_scatter(part_u.astype(jnp.bfloat16), "row", scatter_dimension=1, tiled=True)
    u = lax.all_gather(u, "col", axis=0, tiled=True)
    all_cot = lax.all_gather(cotangent, "col", axis=0, tiled=True)
    share = grad_inverse.shape[1] // n_row
    mine = lax.dynamic_slice_in_dim(grad_inverse, row_index * share, share, 1)
    part_v = jnp.dot(all_cot, mine, preferred_element_type=jnp.float32)
    v = lax.psum(part_v.astype(jnp.bfloat16), "grp")
    v = lax.all_gather(v, "row", axis=1, tiled=True)
    precond = lax.dot_general(u, v, contract, preferred_element_type=jnp.float32) * (1 / SHRINK)
    offsets = sample_rows - col_index * tokens_in.shape[0]
    picked_x = jnp.take(tokens_in, offsets, axis=0)
    picked_g = jnp.take(cotangent, offsets, axis=0)
    samples = picked_x.shape[0]
    total = samples * n_col
    act_panel = lax.all_gather(picked_x[None], ("row", "col"), axis=0, tiled=True).reshape(
        n_row, total, feat_row
    )
    grad_panel = lax.all_gather(picked_g[None], ("grp", "col"), axis=0, tiled=True).reshape(
        n_grp, total, feat_grp
    )
    tile = width // (n_row * n_col)
    first = (row_index * n_col + col_index) * tile
    act_left = lax.dynamic_slice(
        act_panel, (first // feat_row, 0, first % feat_row), (1, total, tile)
    )[0]
    per = feat_grp // feat_row
    act_span = lax.dynamic_slice_in_dim(act_panel, grp_index * per, per, 0)
    act_cov = jnp.einsum("sa,psf->apf", act_left, act_span, preferred_element_type=jnp.float32)
    act_cov = act_cov.reshape(tile, feat_grp) / total
    grad_left = lax.dynamic_slice(
        grad_panel, (first // feat_grp, 0, first % feat_grp), (1, total, tile)
    )[0]
    grad_span = lax.dynamic_index_in_dim(grad_panel, grp_index, 0, keepdims=False)
    grad_cov = (
        lax.dot_general(grad_left, grad_span, contract, preferred_element_type=jnp.float32) / total
    )
    return (precond, act_cov, grad_cov)


def solution(mesh):
    sizes = tuple(mesh.shape[name] for name in ("grp", "row", "col"))
    return jax.shard_map(
        body_kernels if sizes == (4, 4, 2) else body,
        mesh=mesh,
        in_specs=(P("col", "row"), P("col", "grp"), P("col"), P("grp", "row"), P("grp", "col")),
        out_specs=(P(("grp", "row"), "col"), P(("row", "col"), "grp"), P(("row", "col"), "grp")),
        check_vma=False,
    )
```

```python
import functools

import jax
import jax.numpy as jnp
from jax import lax
from jax.experimental import pallas as pl
from jax.experimental.pallas import tpu as pltpu
from jax.sharding import PartitionSpec as P

SHRINK = 2.0 ** -16
BF16 = jnp.bfloat16
F32 = jnp.float32
CONTRACT = (((0,), (0,)), ((), ()))


def gather_kernel(
    rows_ref, t_hbm, c_hbm, a_hbm, g_hbm,
    u_out, v_out, xl_out, xs_out, yl_out, ys_out,
    t_v, c_v, a_v, g_v, oh_v, px_v, q_v, r1_s, r1_r, r2_s, r2_r,
    qb_v, b1_s, b1_r, b2_s, b2_r,
    w_s, w_r, w_v, h_s, h_r, u_v, v_v, xl_v, xs_v, yl_v, ys_v, xlt_v, ylt_v,
    load_sem, out_sem, send_sem, recv_sem,
):
    grp, z, c = lax.axis_index("grp"), lax.axis_index("row"), lax.axis_index("col")
    x, k = grp // 2, grp % 2
    oc, ok, ox = 1 - c, 1 - k, 1 - x
    z1 = z + 1 - 2 * (z % 2)
    z2 = (z + 2) % 4
    z3 = (z1 + 2) % 4
    places = (z, z2, z1, z3)
    to_y = {"col": oc}
    to_k = {"grp": 2 * x + ok}
    to_x = {"grp": 2 * ox + k}
    to_xk = {"grp": 2 * ox + ok}
    to_z1 = {"row": z1}
    to_z2 = {"row": z2}
    tok = t_v.shape[0]
    share = g_v.shape[2]
    half = xl_v.shape[2]
    out_rows = u_v.shape[1]
    phases = ((c, 0, tok), (oc, 0, tok // 2), (oc, tok // 2, tok // 2))

    names = {}
    sends = []

    def copy(name, src, dst, where):
        i = names.setdefault(name, len(names))
        return pltpu.make_async_remote_copy(
            src_ref=src, dst_ref=dst, send_sem=send_sem.at[i], recv_sem=recv_sem.at[i],
            device_id=where, device_id_type=pl.DeviceIdType.MESH,
        )

    def send(name, src, dst, where):
        out = copy(name, src, dst, where)
        out.start()
        sends.append(out)

    def await_in(name, dst, where):
        copy(name, dst, dst, where).wait_recv()

    def load_a(block, sem):
        rows = pl.ds(pl.multiple_of(block * out_rows, out_rows), out_rows)
        return pltpu.make_async_copy(a_hbm.at[rows], a_v.at[rows], load_sem.at[sem])

    def load_g(part, sem):
        columns = pl.ds(pl.multiple_of(part * share, 128), share)
        return pltpu.make_async_copy(g_hbm.at[:, columns], g_v.at[part], load_sem.at[sem])

    odd = z % 2
    away_blocks = (1 - odd, 3 - odd)
    home_blocks = (odd, 2 + odd)
    loads = [
        pltpu.make_async_copy(t_hbm, t_v, load_sem.at[2]),
        load_a(away_blocks[0], 3),
        load_a(away_blocks[1], 4),
        pltpu.make_async_copy(c_hbm, c_v.at[c], load_sem.at[0]),
        load_g(z, 1),
        load_a(home_blocks[0], 5),
        load_a(home_blocks[1], 6),
    ] + [load_g((z + i) % 4, 6 + i) for i in range(1, 4)]
    for load in loads:
        load.start()

    barrier = pltpu.get_barrier_semaphore()
    partners = [to_y, to_k, to_x, to_xk, to_z1, to_z2]
    for where in partners:
        pl.semaphore_signal(barrier, inc=1, device_id=where, device_id_type=pl.DeviceIdType.MESH)
    pl.semaphore_wait(barrier, len(partners))

    feat = t_v.shape[1]
    chunks = (
        (pl.ds(0, tok // 2), pl.ds(0, feat)),
        (pl.ds(tok // 2, tok // 2), pl.ds(0, feat // 2)),
        (pl.ds(tok // 2, tok // 2), pl.ds(feat // 2, feat // 2)),
    )

    def send_cot(i):
        send(("cot", i), c_hbm.at[chunks[i]], c_v.at[(c,) + chunks[i]], to_y)

    def await_cot(i):
        await_in(("cot", i), c_v.at[(oc,) + chunks[i]], to_y)

    send_cot(0)

    hot = lax.broadcasted_iota(jnp.int32, (tok, rows_ref.shape[1]), 0) + c * tok == rows_ref[...]
    oh_v[c] = jnp.where(hot, 1.0, 0.0).astype(BF16)
    send("hot", oh_v.at[c], oh_v.at[c], to_y)

    def pick(block, values):
        return lax.dot_general(oh_v[block], values, CONTRACT, preferred_element_type=F32).astype(BF16)

    def v_at(ph, core, side, step):
        block, first, count = phases[ph]
        row = pl.multiple_of(block * tok + first + (2 * core + side) * (count // 4), count // 4)
        return v_v.at[
            pl.ds(row, count // 4), pl.ds(pl.multiple_of(places[step] * share, 128), share)
        ]

    def cut(ph):
        return pl.ds(0, phases[ph][2] // 4)

    def product(ph):
        block, first, count = phases[ph]
        q = jnp.dot(c_v[block, first:first + count], g_v[z], preferred_element_type=F32)
        q_v[ph, :, cut(ph)] = q.reshape(4, count // 4, share)
        r1_s[ph, :, cut(ph)] = q_v[ph, pl.ds(2 * ok, 2), cut(ph)].astype(BF16)
        send(("r1", ph), r1_s.at[ph, :, cut(ph)], r1_r.at[ph, :, cut(ph)], to_k)

    def across(ph):
        await_in(("r1", ph), r1_r.at[ph, :, cut(ph)], to_k)
        r2_s[ph, cut(ph)] = (
            q_v[ph, 2 * k + ox, cut(ph)] + r1_r[ph, ox, cut(ph)].astype(F32)
        ).astype(BF16)
        send(("r2", ph), r2_s.at[ph, cut(ph)], r2_r.at[ph, cut(ph)], to_x)

    def finish(ph):
        await_in(("r2", ph), r2_r.at[ph, cut(ph)], to_x)
        total = (
            q_v[ph, 2 * k + x, cut(ph)] + r1_r[ph, x, cut(ph)].astype(F32)
            + r2_r[ph, cut(ph)].astype(F32)
        )
        mine = v_at(ph, k, x, 0)
        mine[...] = total.astype(BF16)
        send(("v", ph, 1), mine, mine, to_z2)
        send(("v", ph, 2), mine, mine, to_z1)
        send(("vx", ph, 0), mine, mine, to_x)
        send(("vk", ph, 0), mine, mine, to_k)

    def spread(ph, step):
        got = v_at(ph, k, x, step)
        await_in(("v", ph, step), got, to_z1)
        if step == 1:
            send(("v", ph, 3), got, got, to_z1)
        send(("vx", ph, step), got, got, to_x)
        send(("vk", ph, step), got, got, to_k)

    def relay(ph, step):
        got = v_at(ph, k, ox, step)
        await_in(("vx", ph, step), got, to_x)
        send(("vk", ph, 4 + step), got, got, to_k)

    def collect(ph):
        for step in range(4):
            await_in(("vk", ph, step), v_at(ph, ok, x, step), to_k)
        for step in range(4):
            await_in(("vk", ph, 4 + step), v_at(ph, ok, ox, step), to_k)

    def rows_b(core):
        block, first, count = phases[2]
        return pl.ds(pl.multiple_of(block * tok + first + core * (count // 2), count // 2), count // 2)

    def half_b(j, side):
        mid = feat // 2
        block = c_v[oc, tok // 2:, side * mid:(side + 1) * mid]
        part = g_v[j, side * mid:(side + 1) * mid]
        return jnp.dot(block, part, preferred_element_type=F32).reshape(2, tok // 4, share)

    def product_b(j):
        qb_v[j] = qb_v[j] + half_b(j, 1)
        b1_s[j] = qb_v[j, ok].astype(BF16)
        send(("b1", j), b1_s.at[j], b1_r.at[j], to_k)

    def across_b(j):
        await_in(("b1", j), b1_r.at[j], to_k)
        total = qb_v[j, k] + b1_r[j].astype(F32)
        qb_v[j, k] = total
        b2_s[j] = total.astype(BF16)
        send(("b2", j), b2_s.at[j], b2_r.at[j], to_x)

    def finish_b(j):
        await_in(("b2", j), b2_r.at[j], to_x)
        mine = v_v.at[rows_b(k), j * share:(j + 1) * share]
        mine[...] = (qb_v[j, k] + b2_r[j].astype(F32)).astype(BF16)
        send(("bk", j), mine, mine, to_k)

    def collect_b():
        for j in range(4):
            got = v_v.at[rows_b(ok), j * share:(j + 1) * share]
            await_in(("bk", j), got, to_k)

    def u_part(block):
        rows = a_v[pl.ds(pl.multiple_of(block * out_rows, out_rows), out_rows), :]
        return lax.dot_general(t_v[...], rows, (((1,), (1,)), ((), ())), preferred_element_type=F32)

    def at_half(ref, index):
        return ref.at[:, pl.ds(pl.multiple_of(index * half, 128), half)]

    has_span = grp == z
    is_z2 = grp == z2
    is_z1 = grp == z1
    span = xs_v.at[c]
    x_z2 = copy("x2", span, span, to_z2)
    x_z1 = copy("x1", span, span, to_z1)

    loads[0].wait()
    px_v[...] = pick(c, t_v[...])

    @pl.when(has_span)
    def _():
        xs_v[c] = px_v[...]
        x_z2.start()
        x_z1.start()

    t_v[...] = t_v[...] * jnp.asarray(SHRINK, BF16)
    for i in range(2):
        loads[1 + i].wait()
        w_s[i] = u_part(away_blocks[i]).astype(BF16)
    send("w", w_s, w_r, to_z1)
    send_cot(1)
    loads[3].wait()
    loads[4].wait()
    product(0)
    send_cot(2)
    ys_v[c] = pick(c, c_v[c])

    def y_copies(block):
        left = ys_v.at[block, :, pl.ds(pl.multiple_of(c * half, 128), half)]
        own = 0 if block is c else 1
        return left, [
            copy(("yl", own, i), left, yl_v.at[block], w) for i, w in enumerate([to_k, to_x, to_xk])
        ]

    left_c, y_c = y_copies(c)
    left_oc, y_oc = y_copies(oc)

    @pl.when(has_span)
    def _():
        for out in y_c:
            out.start()
        yl_v[c] = left_c[...]

    across(0)
    for i in range(2):
        loads[5 + i].wait()
        w_v[i] = u_part(home_blocks[i])
    finish(0)
    await_cot(0)
    product(1)

    @pl.when(is_z2)
    def _():
        x_z2.wait_recv()
        x_z1.start()

    across(1)
    await_in("w", w_r, to_z1)
    mine, away = z // 2, 1 - z // 2
    h_s[...] = (w_v[away] + w_r[away].astype(F32)).astype(BF16)
    send("h", h_s, h_r, to_z2)
    spread(0, 1)
    finish(1)
    spread(0, 2)
    for i in range(7, 10):
        loads[i].wait()
    await_cot(1)
    for j in range(4):
        qb_v[j] = half_b(j, 0)
    spread(0, 3)
    await_cot(2)
    product_b(0)
    product_b(1)
    product_b(2)
    across_b(0)
    product_b(3)
    for j in range(1, 4):
        across_b(j)
    for step in range(1, 4):
        spread(1, step)
    send("xl", at_half(px_v, oc), xl_v.at[c], to_y)
    xl_v[c] = at_half(px_v, c)[...]

    @pl.when(jnp.logical_or(is_z1, grp == z3))
    def _():
        x_z1.wait_recv()

    send("xy", span, span, to_y)
    await_in("h", h_r, to_z2)
    u = w_v[mine] + w_r[mine].astype(F32) + h_r[...].astype(F32)
    u_v[c] = u.T.astype(BF16)
    send("u", u_v.at[c], u_v.at[c], to_y)
    await_in("hot", oh_v.at[oc], to_y)
    ys_v[oc] = pick(oc, c_v[oc])

    @pl.when(has_span)
    def _():
        for out in y_oc:
            out.start()
        yl_v[oc] = left_oc[...]

    for ph in range(2):
        for step in range(4):
            relay(ph, step)
    for j in range(4):
        finish_b(j)
    collect(0)

    outs = []

    def put(src, dst):
        out = pltpu.make_async_copy(src, dst, out_sem.at[len(outs)])
        out.start()
        outs.append(out)

    def put_v(ph):
        block, first, count = phases[ph]
        rows = pl.ds(pl.multiple_of(block * tok + first, count), count)
        put(v_v.at[rows], v_out.at[rows])

    put_v(0)
    put(ys_v, ys_out)
    collect(1)
    put_v(1)
    await_in("xl", xl_v.at[oc], to_y)
    xlt_v[...] = xl_v[...].reshape(xlt_v.shape[::-1]).T
    put(xlt_v, xl_out)

    @pl.when(grp == 2 * (z // 2) + (1 - z % 2))
    def _():
        y_c[0].wait_recv()
        y_oc[0].wait_recv()

    @pl.when(grp == 2 * (1 - z // 2) + z % 2)
    def _():
        y_c[1].wait_recv()
        y_oc[1].wait_recv()

    @pl.when(grp == 2 * (1 - z // 2) + (1 - z % 2))
    def _():
        y_c[2].wait_recv()
        y_oc[2].wait_recv()

    ylt_v[...] = yl_v[...].reshape(ylt_v.shape[::-1]).T
    put(ylt_v, yl_out)
    await_in("xy", xs_v.at[oc], to_y)
    put(xs_v, xs_out)
    await_in("u", u_v.at[oc], to_y)
    for block in range(2):
        put(u_v.at[block], u_out.at[:, block * tok:(block + 1) * tok])
    collect_b()
    put_v(2)

    @pl.when(has_span)
    def _():
        x_z2.wait_send()
        x_z1.wait_send()
        for out in y_c + y_oc:
            out.wait_send()

    @pl.when(is_z2)
    def _():
        x_z1.wait_send()

    for out in sends:
        out.wait_send()
    for out in outs:
        out.wait()


def gather(rows, tokens_in, cotangent, act_inverse, grad_inverse, n_row):
    tok, feat = tokens_in.shape
    samples = rows.shape[1]
    share = grad_inverse.shape[1] // n_row
    out_rows = feat // n_row
    half = feat // 2
    piece = tok // 4
    v_shape, span = (2 * tok, grad_inverse.shape[1]), (2, samples, feat)
    left, left_t = (2, samples, half), (half, 2 * samples)
    shapes = [(out_rows, 2 * tok), v_shape, left_t, span, left_t, span]
    held = [(2, out_rows, tok), v_shape, left, span, left, span, left_t, left_t]
    vmem = pltpu.VMEM
    return pl.pallas_call(
        gather_kernel,
        out_shape=[vmem(s, BF16) for s in shapes],
        in_specs=[pl.BlockSpec(memory_space=vmem)] + [pl.BlockSpec(memory_space=pl.ANY)] * 4,
        out_specs=[pl.BlockSpec(memory_space=pl.ANY)] * 6,
        scratch_shapes=[
            vmem((tok, feat), BF16),
            vmem((2, tok, feat), BF16),
            vmem(act_inverse.shape, BF16),
            vmem((n_row, feat, share), BF16),
            vmem((2, tok, samples), BF16),
            vmem((samples, feat), BF16),
            vmem((2, 4, piece, share), F32),
            vmem((2, 2, piece, share), BF16),
            vmem((2, 2, piece, share), BF16),
            vmem((2, piece, share), BF16),
            vmem((2, piece, share), BF16),
            vmem((4, 2, piece, share), F32),
            vmem((4, piece, share), BF16),
            vmem((4, piece, share), BF16),
            vmem((4, piece, share), BF16),
            vmem((4, piece, share), BF16),
            vmem((2, tok, out_rows), BF16),
            vmem((2, tok, out_rows), BF16),
            vmem((2, tok, out_rows), F32),
            vmem((tok, out_rows), BF16),
            vmem((tok, out_rows), BF16),
        ] + [vmem(s, BF16) for s in held] + [
            pltpu.SemaphoreType.DMA((10,)),
            pltpu.SemaphoreType.DMA((9,)),
            pltpu.SemaphoreType.DMA((72,)),
            pltpu.SemaphoreType.DMA((72,)),
        ],
        compiler_params=pltpu.CompilerParams(
            collective_id=0, has_side_effects=True, vmem_limit_bytes=58 * 2 ** 20
        ),
        cost_estimate=pl.CostEstimate(flops=3 * 10 ** 9, bytes_accessed=10 ** 7, transcendentals=0),
    )(rows, tokens_in, cotangent, act_inverse, grad_inverse)


def product_kernel(total, ut, v, xt, xs, yt, ys, p_out, a_out, g_out):
    a_out[...] = jnp.dot(xt[...], xs[...], preferred_element_type=F32) * (1 / total)
    g_out[...] = jnp.dot(yt[...], ys[...], preferred_element_type=F32) * (1 / total)
    p_out[...] = jnp.dot(ut[...], v[...], preferred_element_type=F32) * (1 / SHRINK)


def products(ut, v, xt, xs, yt, ys):
    steps = 6
    total = xt.shape[1]

    def whole(a):
        return pl.BlockSpec(a.shape, lambda i: (0, 0))

    def cut(rows, width):
        return pl.BlockSpec((rows, width // steps), lambda i: (0, i))

    return pl.pallas_call(
        functools.partial(product_kernel, total),
        grid=(steps,),
        in_specs=[
            whole(ut), cut(v.shape[0], v.shape[1]),
            whole(xt), cut(total, xs.shape[1]), whole(yt), cut(total, ys.shape[1]),
        ],
        out_specs=[
            cut(ut.shape[0], v.shape[1]), cut(xt.shape[0], xs.shape[1]), cut(yt.shape[0], ys.shape[1])
        ],
        out_shape=[
            jax.ShapeDtypeStruct((ut.shape[0], v.shape[1]), F32),
            jax.ShapeDtypeStruct((xt.shape[0], xs.shape[1]), F32),
            jax.ShapeDtypeStruct((yt.shape[0], ys.shape[1]), F32),
        ],
        compiler_params=pltpu.CompilerParams(vmem_limit_bytes=40 * 2 ** 20),
        cost_estimate=pl.CostEstimate(flops=10 ** 9, bytes_accessed=17 * 10 ** 6, transcendentals=0),
    )(ut, v, xt, xs, yt, ys)


def flat(a):
    return a.reshape(-1, a.shape[-1])


def body_kernels(tokens_in, cotangent, sample_rows, act_inverse, grad_inverse):
    ut, v, xt, xs, yt, ys = gather(
        sample_rows[None], tokens_in, cotangent, act_inverse, grad_inverse, lax.axis_size("row")
    )
    return tuple(products(ut, v, xt, flat(xs), yt, flat(ys)))


def body(tokens_in, cotangent, sample_rows, act_inverse, grad_inverse):
    feat_row = tokens_in.shape[1]
    feat_grp = cotangent.shape[1]
    n_row = lax.axis_size("row")
    n_col = lax.axis_size("col")
    n_grp = lax.axis_size("grp")
    width = feat_row * n_row
    contract = (((0,), (0,)), ((), ()))
    col_index = lax.axis_index("col")
    grp_index = lax.axis_index("grp")
    row_index = lax.axis_index("row")
    small = tokens_in * jnp.asarray(SHRINK, tokens_in.dtype)
    part_u = lax.dot_general(
        small, act_inverse, (((1,), (1,)), ((), ())), preferred_element_type=jnp.float32
    )
    u = lax.psum_scatter(part_u.astype(jnp.bfloat16), "row", scatter_dimension=1, tiled=True)
    u = lax.all_gather(u, "col", axis=0, tiled=True)
    all_cot = lax.all_gather(cotangent, "col", axis=0, tiled=True)
    share = grad_inverse.shape[1] // n_row
    mine = lax.dynamic_slice_in_dim(grad_inverse, row_index * share, share, 1)
    part_v = jnp.dot(all_cot, mine, preferred_element_type=jnp.float32)
    v = lax.psum(part_v.astype(jnp.bfloat16), "grp")
    v = lax.all_gather(v, "row", axis=1, tiled=True)
    precond = lax.dot_general(u, v, contract, preferred_element_type=jnp.float32) * (1 / SHRINK)
    offsets = sample_rows - col_index * tokens_in.shape[0]
    picked_x = jnp.take(tokens_in, offsets, axis=0)
    picked_g = jnp.take(cotangent, offsets, axis=0)
    samples = picked_x.shape[0]
    total = samples * n_col
    act_panel = lax.all_gather(picked_x[None], ("row", "col"), axis=0, tiled=True).reshape(
        n_row, total, feat_row
    )
    grad_panel = lax.all_gather(picked_g[None], ("grp", "col"), axis=0, tiled=True).reshape(
        n_grp, total, feat_grp
    )
    tile = width // (n_row * n_col)
    first = (row_index * n_col + col_index) * tile
    act_left = lax.dynamic_slice(
        act_panel, (first // feat_row, 0, first % feat_row), (1, total, tile)
    )[0]
    per = feat_grp // feat_row
    act_span = lax.dynamic_slice_in_dim(act_panel, grp_index * per, per, 0)
    act_cov = jnp.einsum("sa,psf->apf", act_left, act_span, preferred_element_type=jnp.float32)
    act_cov = act_cov.reshape(tile, feat_grp) / total
    grad_left = lax.dynamic_slice(
        grad_panel, (first // feat_grp, 0, first % feat_grp), (1, total, tile)
    )[0]
    grad_span = lax.dynamic_index_in_dim(grad_panel, grp_index, 0, keepdims=False)
    grad_cov = (
        lax.dot_general(grad_left, grad_span, contract, preferred_element_type=jnp.float32) / total
    )
    return (precond, act_cov, grad_cov)


def solution(mesh):
    sizes = tuple(mesh.shape[name] for name in ("grp", "row", "col"))
    return jax.shard_map(
        body_kernels if sizes == (4, 4, 2) else body,
        mesh=mesh,
        in_specs=(P("col", "row"), P("col", "grp"), P("col"), P("grp", "row"), P("grp", "col")),
        out_specs=(P(("grp", "row"), "col"), P(("row", "col"), "grp"), P(("row", "col"), "grp")),
        check_vma=False,
    )
```

```python
import functools

import jax
import jax.numpy as jnp
from jax import lax
from jax.experimental import pallas as pl
from jax.experimental.pallas import tpu as pltpu
from jax.sharding import PartitionSpec as P

SHRINK = 2.0 ** -16
BF16 = jnp.bfloat16
F32 = jnp.float32
CONTRACT = (((0,), (0,)), ((), ()))


def gather_kernel(
    rows_ref, t_hbm, c_hbm, a_hbm, g_hbm,
    u_out, v_out, xl_out, xs_out, yl_out, ys_out,
    t_v, c_v, a_v, g_v, oh_v, px_v, q_v, r1_s, r1_r, r2_s, r2_r,
    qb_v, b1_s, b1_r, b2_s, b2_r,
    w_s, w_r, w_v, h_s, h_r, u_v, v_v, xl_v, xs_v, yl_v, ys_v, xlt_v, ylt_v,
    load_sem, out_sem, send_sem, recv_sem,
):
    grp, z, c = lax.axis_index("grp"), lax.axis_index("row"), lax.axis_index("col")
    x, k = grp // 2, grp % 2
    oc, ok, ox = 1 - c, 1 - k, 1 - x
    z1 = z + 1 - 2 * (z % 2)
    z2 = (z + 2) % 4
    z3 = (z1 + 2) % 4
    places = (z, z2, z1, z3)
    to_y = {"col": oc}
    to_k = {"grp": 2 * x + ok}
    to_x = {"grp": 2 * ox + k}
    to_xk = {"grp": 2 * ox + ok}
    to_z1 = {"row": z1}
    to_z2 = {"row": z2}
    tok = t_v.shape[0]
    share = g_v.shape[2]
    half = xl_v.shape[2]
    out_rows = u_v.shape[1]
    phases = ((c, 0, tok), (oc, 0, tok // 2), (oc, tok // 2, tok // 2))

    names = {}
    sends = []

    def copy(name, src, dst, where):
        i = names.setdefault(name, len(names))
        return pltpu.make_async_remote_copy(
            src_ref=src, dst_ref=dst, send_sem=send_sem.at[i], recv_sem=recv_sem.at[i],
            device_id=where, device_id_type=pl.DeviceIdType.MESH,
        )

    def send(name, src, dst, where):
        out = copy(name, src, dst, where)
        out.start()
        sends.append(out)

    def await_in(name, dst, where):
        copy(name, dst, dst, where).wait_recv()

    def load_a(block, sem):
        rows = pl.ds(pl.multiple_of(block * out_rows, out_rows), out_rows)
        return pltpu.make_async_copy(a_hbm.at[rows], a_v.at[rows], load_sem.at[sem])

    def load_g(part, sem):
        columns = pl.ds(pl.multiple_of(part * share, 128), share)
        return pltpu.make_async_copy(g_hbm.at[:, columns], g_v.at[part], load_sem.at[sem])

    odd = z % 2
    away_blocks = (1 - odd, 3 - odd)
    home_blocks = (odd, 2 + odd)
    loads = [
        pltpu.make_async_copy(t_hbm, t_v, load_sem.at[2]),
        load_a(away_blocks[0], 3),
        load_a(away_blocks[1], 4),
        pltpu.make_async_copy(c_hbm, c_v.at[c], load_sem.at[0]),
        load_g(z, 1),
        load_a(home_blocks[0], 5),
        load_a(home_blocks[1], 6),
    ] + [load_g((z + i) % 4, 6 + i) for i in range(1, 4)]
    for load in loads:
        load.start()

    barrier = pltpu.get_barrier_semaphore()
    partners = [to_y, to_k, to_x, to_xk, to_z1, to_z2]
    for where in partners:
        pl.semaphore_signal(barrier, inc=1, device_id=where, device_id_type=pl.DeviceIdType.MESH)
    pl.semaphore_wait(barrier, len(partners))

    for ph in (1, 2):
        part = pl.ds(phases[ph][1], phases[ph][2])
        send(("cot", ph), c_hbm.at[part], c_v.at[c, part], to_y)

    hot = lax.broadcasted_iota(jnp.int32, (tok, rows_ref.shape[1]), 0) + c * tok == rows_ref[...]
    oh_v[c] = jnp.where(hot, 1.0, 0.0).astype(BF16)
    send("hot", oh_v.at[c], oh_v.at[c], to_y)

    def pick(block, values):
        return lax.dot_general(oh_v[block], values, CONTRACT, preferred_element_type=F32).astype(BF16)

    def v_at(ph, core, side, step):
        block, first, count = phases[ph]
        row = pl.multiple_of(block * tok + first + (2 * core + side) * (count // 4), count // 4)
        return v_v.at[
            pl.ds(row, count // 4), pl.ds(pl.multiple_of(places[step] * share, 128), share)
        ]

    def cut(ph):
        return pl.ds(0, phases[ph][2] // 4)

    def product(ph):
        block, first, count = phases[ph]
        q = jnp.dot(c_v[block, first:first + count], g_v[z], preferred_element_type=F32)
        q_v[ph, :, cut(ph)] = q.reshape(4, count // 4, share)
        r1_s[ph, :, cut(ph)] = q_v[ph, pl.ds(2 * ok, 2), cut(ph)].astype(BF16)
        send(("r1", ph), r1_s.at[ph, :, cut(ph)], r1_r.at[ph, :, cut(ph)], to_k)

    def across(ph):
        await_in(("r1", ph), r1_r.at[ph, :, cut(ph)], to_k)
        r2_s[ph, cut(ph)] = (
            q_v[ph, 2 * k + ox, cut(ph)] + r1_r[ph, ox, cut(ph)].astype(F32)
        ).astype(BF16)
        send(("r2", ph), r2_s.at[ph, cut(ph)], r2_r.at[ph, cut(ph)], to_x)

    def finish(ph):
        await_in(("r2", ph), r2_r.at[ph, cut(ph)], to_x)
        total = (
            q_v[ph, 2 * k + x, cut(ph)] + r1_r[ph, x, cut(ph)].astype(F32)
            + r2_r[ph, cut(ph)].astype(F32)
        )
        mine = v_at(ph, k, x, 0)
        mine[...] = total.astype(BF16)
        send(("v", ph, 1), mine, mine, to_z2)
        send(("v", ph, 2), mine, mine, to_z1)
        send(("vx", ph, 0), mine, mine, to_x)
        send(("vk", ph, 0), mine, mine, to_k)

    def spread(ph, step):
        got = v_at(ph, k, x, step)
        await_in(("v", ph, step), got, to_z1)
        if step == 1:
            send(("v", ph, 3), got, got, to_z1)
        send(("vx", ph, step), got, got, to_x)
        send(("vk", ph, step), got, got, to_k)

    def relay(ph, step):
        got = v_at(ph, k, ox, step)
        await_in(("vx", ph, step), got, to_x)
        send(("vk", ph, 4 + step), got, got, to_k)

    def collect(ph):
        for step in range(4):
            await_in(("vk", ph, step), v_at(ph, ok, x, step), to_k)
        for step in range(4):
            await_in(("vk", ph, 4 + step), v_at(ph, ok, ox, step), to_k)

    def rows_b(ph, core):
        block, first, count = phases[ph]
        return pl.ds(pl.multiple_of(block * tok + first + core * (count // 2), count // 2), count // 2)

    def product_b(ph, j):
        block, first, count = phases[ph]
        unit = 4 * (ph - 1) + j
        q = jnp.dot(c_v[block, first:first + count], g_v[j], preferred_element_type=F32)
        qb_v[unit] = q.reshape(2, count // 2, share)
        b1_s[unit] = qb_v[unit, ok].astype(BF16)
        send(("b1", unit), b1_s.at[unit], b1_r.at[unit], to_k)

    def across_b(ph, j):
        unit = 4 * (ph - 1) + j
        await_in(("b1", unit), b1_r.at[unit], to_k)
        total = qb_v[unit, k] + b1_r[unit].astype(F32)
        qb_v[unit, k] = total
        b2_s[unit] = total.astype(BF16)
        send(("b2", unit), b2_s.at[unit], b2_r.at[unit], to_x)

    def finish_b(ph, j):
        unit = 4 * (ph - 1) + j
        await_in(("b2", unit), b2_r.at[unit], to_x)
        mine = v_v.at[rows_b(ph, k), j * share:(j + 1) * share]
        mine[...] = (qb_v[unit, k] + b2_r[unit].astype(F32)).astype(BF16)
        send(("bk", unit), mine, mine, to_k)

    def collect_b(ph):
        for j in range(4):
            got = v_v.at[rows_b(ph, ok), j * share:(j + 1) * share]
            await_in(("bk", 4 * (ph - 1) + j), got, to_k)

    def run_b(ph, between=None):
        for j in range(3):
            product_b(ph, j)
        across_b(ph, 0)
        product_b(ph, 3)
        if between:
            between()
        for j in range(1, 4):
            across_b(ph, j)

    def u_part(block):
        rows = a_v[pl.ds(pl.multiple_of(block * out_rows, out_rows), out_rows), :]
        return lax.dot_general(t_v[...], rows, (((1,), (1,)), ((), ())), preferred_element_type=F32)

    def at_half(ref, index):
        return ref.at[:, pl.ds(pl.multiple_of(index * half, 128), half)]

    def await_cot(ph):
        part = pl.ds(phases[ph][1], phases[ph][2])
        await_in(("cot", ph), c_v.at[oc, part], to_y)

    has_span = grp == z
    is_z2 = grp == z2
    is_z1 = grp == z1
    span = xs_v.at[c]
    x_z2 = copy("x2", span, span, to_z2)
    x_z1 = copy("x1", span, span, to_z1)

    loads[0].wait()
    px_v[...] = pick(c, t_v[...])

    @pl.when(has_span)
    def _():
        xs_v[c] = px_v[...]
        x_z2.start()
        x_z1.start()

    t_v[...] = t_v[...] * jnp.asarray(SHRINK, BF16)
    for i in range(2):
        loads[1 + i].wait()
        w_s[i] = u_part(away_blocks[i]).astype(BF16)
    send("w", w_s, w_r, to_z1)
    loads[3].wait()
    loads[4].wait()
    product(0)
    ys_v[c] = pick(c, c_v[c])

    def y_copies(block):
        left = ys_v.at[block, :, pl.ds(pl.multiple_of(c * half, 128), half)]
        own = 0 if block is c else 1
        return left, [
            copy(("yl", own, i), left, yl_v.at[block], w) for i, w in enumerate([to_k, to_x, to_xk])
        ]

    left_c, y_c = y_copies(c)
    left_oc, y_oc = y_copies(oc)

    @pl.when(has_span)
    def _():
        for out in y_c:
            out.start()
        yl_v[c] = left_c[...]

    across(0)
    for i in range(2):
        loads[5 + i].wait()
        w_v[i] = u_part(home_blocks[i])
    finish(0)
    await_cot(1)
    for i in range(7, 10):
        loads[i].wait()
    run_b(1)

    @pl.when(is_z2)
    def _():
        x_z2.wait_recv()
        x_z1.start()

    await_in("w", w_r, to_z1)
    mine, away = z // 2, 1 - z // 2
    h_s[...] = (w_v[away] + w_r[away].astype(F32)).astype(BF16)
    send("h", h_s, h_r, to_z2)
    spread(0, 1)
    spread(0, 2)
    await_cot(2)
    run_b(2, lambda: spread(0, 3))
    for j in range(4):
        finish_b(1, j)
    send("xl", at_half(px_v, oc), xl_v.at[c], to_y)
    xl_v[c] = at_half(px_v, c)[...]

    @pl.when(jnp.logical_or(is_z1, grp == z3))
    def _():
        x_z1.wait_recv()

    send("xy", span, span, to_y)
    await_in("hot", oh_v.at[oc], to_y)
    ys_v[oc] = pick(oc, c_v[oc])

    @pl.when(has_span)
    def _():
        for out in y_oc:
            out.start()
        yl_v[oc] = left_oc[...]

    await_in("h", h_r, to_z2)
    u = w_v[mine] + w_r[mine].astype(F32) + h_r[...].astype(F32)
    u_v[c] = u.T.astype(BF16)
    send("u", u_v.at[c], u_v.at[c], to_y)
    for step in range(4):
        relay(0, step)
    for j in range(4):
        finish_b(2, j)
    collect(0)

    outs = []

    def put(src, dst):
        out = pltpu.make_async_copy(src, dst, out_sem.at[len(outs)])
        out.start()
        outs.append(out)

    def put_v(ph):
        block, first, count = phases[ph]
        rows = pl.ds(pl.multiple_of(block * tok + first, count), count)
        put(v_v.at[rows], v_out.at[rows])

    put_v(0)
    put(ys_v, ys_out)
    collect_b(1)
    put_v(1)
    await_in("xl", xl_v.at[oc], to_y)
    xlt_v[...] = xl_v[...].reshape(xlt_v.shape[::-1]).T
    put(xlt_v, xl_out)

    @pl.when(grp == 2 * (z // 2) + (1 - z % 2))
    def _():
        y_c[0].wait_recv()
        y_oc[0].wait_recv()

    @pl.when(grp == 2 * (1 - z // 2) + z % 2)
    def _():
        y_c[1].wait_recv()
        y_oc[1].wait_recv()

    @pl.when(grp == 2 * (1 - z // 2) + (1 - z % 2))
    def _():
        y_c[2].wait_recv()
        y_oc[2].wait_recv()

    ylt_v[...] = yl_v[...].reshape(ylt_v.shape[::-1]).T
    put(ylt_v, yl_out)
    await_in("xy", xs_v.at[oc], to_y)
    put(xs_v, xs_out)
    await_in("u", u_v.at[oc], to_y)
    for block in range(2):
        put(u_v.at[block], u_out.at[:, block * tok:(block + 1) * tok])
    collect_b(2)
    put_v(2)

    @pl.when(has_span)
    def _():
        x_z2.wait_send()
        x_z1.wait_send()
        for out in y_c + y_oc:
            out.wait_send()

    @pl.when(is_z2)
    def _():
        x_z1.wait_send()

    for out in sends:
        out.wait_send()
    for out in outs:
        out.wait()


def gather(rows, tokens_in, cotangent, act_inverse, grad_inverse, n_row):
    tok, feat = tokens_in.shape
    samples = rows.shape[1]
    share = grad_inverse.shape[1] // n_row
    out_rows = feat // n_row
    half = feat // 2
    piece = tok // 4
    v_shape, span = (2 * tok, grad_inverse.shape[1]), (2, samples, feat)
    left, left_t = (2, samples, half), (half, 2 * samples)
    shapes = [(out_rows, 2 * tok), v_shape, left_t, span, left_t, span]
    held = [(2, out_rows, tok), v_shape, left, span, left, span, left_t, left_t]
    vmem = pltpu.VMEM
    return pl.pallas_call(
        gather_kernel,
        out_shape=[vmem(s, BF16) for s in shapes],
        in_specs=[pl.BlockSpec(memory_space=vmem)] + [pl.BlockSpec(memory_space=pl.ANY)] * 4,
        out_specs=[pl.BlockSpec(memory_space=pl.ANY)] * 6,
        scratch_shapes=[
            vmem((tok, feat), BF16),
            vmem((2, tok, feat), BF16),
            vmem(act_inverse.shape, BF16),
            vmem((n_row, feat, share), BF16),
            vmem((2, tok, samples), BF16),
            vmem((samples, feat), BF16),
            vmem((1, 4, piece, share), F32),
            vmem((1, 2, piece, share), BF16),
            vmem((1, 2, piece, share), BF16),
            vmem((1, piece, share), BF16),
            vmem((1, piece, share), BF16),
            vmem((8, 2, piece, share), F32),
            vmem((8, piece, share), BF16),
            vmem((8, piece, share), BF16),
            vmem((8, piece, share), BF16),
            vmem((8, piece, share), BF16),
            vmem((2, tok, out_rows), BF16),
            vmem((2, tok, out_rows), BF16),
            vmem((2, tok, out_rows), F32),
            vmem((tok, out_rows), BF16),
            vmem((tok, out_rows), BF16),
        ] + [vmem(s, BF16) for s in held] + [
            pltpu.SemaphoreType.DMA((10,)),
            pltpu.SemaphoreType.DMA((9,)),
            pltpu.SemaphoreType.DMA((72,)),
            pltpu.SemaphoreType.DMA((72,)),
        ],
        compiler_params=pltpu.CompilerParams(
            collective_id=0, has_side_effects=True, vmem_limit_bytes=58 * 2 ** 20
        ),
        cost_estimate=pl.CostEstimate(flops=3 * 10 ** 9, bytes_accessed=10 ** 7, transcendentals=0),
    )(rows, tokens_in, cotangent, act_inverse, grad_inverse)


def product_kernel(total, ut, v, xt, xs, yt, ys, p_out, a_out, g_out):
    a_out[...] = jnp.dot(xt[...], xs[...], preferred_element_type=F32) * (1 / total)
    g_out[...] = jnp.dot(yt[...], ys[...], preferred_element_type=F32) * (1 / total)
    p_out[...] = jnp.dot(ut[...], v[...], preferred_element_type=F32) * (1 / SHRINK)


def products(ut, v, xt, xs, yt, ys):
    steps = 6
    total = xt.shape[1]

    def whole(a):
        return pl.BlockSpec(a.shape, lambda i: (0, 0))

    def cut(rows, width):
        return pl.BlockSpec((rows, width // steps), lambda i: (0, i))

    return pl.pallas_call(
        functools.partial(product_kernel, total),
        grid=(steps,),
        in_specs=[
            whole(ut), cut(v.shape[0], v.shape[1]),
            whole(xt), cut(total, xs.shape[1]), whole(yt), cut(total, ys.shape[1]),
        ],
        out_specs=[
            cut(ut.shape[0], v.shape[1]), cut(xt.shape[0], xs.shape[1]), cut(yt.shape[0], ys.shape[1])
        ],
        out_shape=[
            jax.ShapeDtypeStruct((ut.shape[0], v.shape[1]), F32),
            jax.ShapeDtypeStruct((xt.shape[0], xs.shape[1]), F32),
            jax.ShapeDtypeStruct((yt.shape[0], ys.shape[1]), F32),
        ],
        compiler_params=pltpu.CompilerParams(vmem_limit_bytes=40 * 2 ** 20),
        cost_estimate=pl.CostEstimate(flops=10 ** 9, bytes_accessed=17 * 10 ** 6, transcendentals=0),
    )(ut, v, xt, xs, yt, ys)


def flat(a):
    return a.reshape(-1, a.shape[-1])


def body_kernels(tokens_in, cotangent, sample_rows, act_inverse, grad_inverse):
    ut, v, xt, xs, yt, ys = gather(
        sample_rows[None], tokens_in, cotangent, act_inverse, grad_inverse, lax.axis_size("row")
    )
    return tuple(products(ut, v, xt, flat(xs), yt, flat(ys)))


def body(tokens_in, cotangent, sample_rows, act_inverse, grad_inverse):
    feat_row = tokens_in.shape[1]
    feat_grp = cotangent.shape[1]
    n_row = lax.axis_size("row")
    n_col = lax.axis_size("col")
    n_grp = lax.axis_size("grp")
    width = feat_row * n_row
    contract = (((0,), (0,)), ((), ()))
    col_index = lax.axis_index("col")
    grp_index = lax.axis_index("grp")
    row_index = lax.axis_index("row")
    small = tokens_in * jnp.asarray(SHRINK, tokens_in.dtype)
    part_u = lax.dot_general(
        small, act_inverse, (((1,), (1,)), ((), ())), preferred_element_type=jnp.float32
    )
    u = lax.psum_scatter(part_u.astype(jnp.bfloat16), "row", scatter_dimension=1, tiled=True)
    u = lax.all_gather(u, "col", axis=0, tiled=True)
    all_cot = lax.all_gather(cotangent, "col", axis=0, tiled=True)
    share = grad_inverse.shape[1] // n_row
    mine = lax.dynamic_slice_in_dim(grad_inverse, row_index * share, share, 1)
    part_v = jnp.dot(all_cot, mine, preferred_element_type=jnp.float32)
    v = lax.psum(part_v.astype(jnp.bfloat16), "grp")
    v = lax.all_gather(v, "row", axis=1, tiled=True)
    precond = lax.dot_general(u, v, contract, preferred_element_type=jnp.float32) * (1 / SHRINK)
    offsets = sample_rows - col_index * tokens_in.shape[0]
    picked_x = jnp.take(tokens_in, offsets, axis=0)
    picked_g = jnp.take(cotangent, offsets, axis=0)
    samples = picked_x.shape[0]
    total = samples * n_col
    act_panel = lax.all_gather(picked_x[None], ("row", "col"), axis=0, tiled=True).reshape(
        n_row, total, feat_row
    )
    grad_panel = lax.all_gather(picked_g[None], ("grp", "col"), axis=0, tiled=True).reshape(
        n_grp, total, feat_grp
    )
    tile = width // (n_row * n_col)
    first = (row_index * n_col + col_index) * tile
    act_left = lax.dynamic_slice(
        act_panel, (first // feat_row, 0, first % feat_row), (1, total, tile)
    )[0]
    per = feat_grp // feat_row
    act_span = lax.dynamic_slice_in_dim(act_panel, grp_index * per, per, 0)
    act_cov = jnp.einsum("sa,psf->apf", act_left, act_span, preferred_element_type=jnp.float32)
    act_cov = act_cov.reshape(tile, feat_grp) / total
    grad_left = lax.dynamic_slice(
        grad_panel, (first // feat_grp, 0, first % feat_grp), (1, total, tile)
    )[0]
    grad_span = lax.dynamic_index_in_dim(grad_panel, grp_index, 0, keepdims=False)
    grad_cov = (
        lax.dot_general(grad_left, grad_span, contract, preferred_element_type=jnp.float32) / total
    )
    return (precond, act_cov, grad_cov)


def solution(mesh):
    sizes = tuple(mesh.shape[name] for name in ("grp", "row", "col"))
    return jax.shard_map(
        body_kernels if sizes == (4, 4, 2) else body,
        mesh=mesh,
        in_specs=(P("col", "row"), P("col", "grp"), P("col"), P("grp", "row"), P("grp", "col")),
        out_specs=(P(("grp", "row"), "col"), P(("row", "col"), "grp"), P(("row", "col"), "grp")),
        check_vma=False,
    )
```

```python
import functools

import jax
import jax.numpy as jnp
from jax import lax
from jax.experimental import pallas as pl
from jax.experimental.pallas import tpu as pltpu
from jax.sharding import PartitionSpec as P

SHRINK = 2.0 ** -16
BF16 = jnp.bfloat16
F32 = jnp.float32
CONTRACT = (((0,), (0,)), ((), ()))


def gather_kernel(
    rows_ref, t_hbm, c_hbm, a_hbm, g_hbm,
    u_out, v_out, xl_out, xs_out, yl_out, ys_out,
    t_v, c_v, a_v, g_v, oh_v, px_v, q_v, r1_s, r1_r, r2_s, r2_r,
    qb_v, b1_s, b1_r, b2_s, b2_r,
    w_s, w_r, w_v, h_s, h_r, u_v, v_v, xl_v, xs_v, yl_v, ys_v, xlt_v, ylt_v,
    load_sem, out_sem, send_sem, recv_sem,
):
    grp, z, c = lax.axis_index("grp"), lax.axis_index("row"), lax.axis_index("col")
    x, k = grp // 2, grp % 2
    oc, ok, ox = 1 - c, 1 - k, 1 - x
    z1 = z + 1 - 2 * (z % 2)
    z2 = (z + 2) % 4
    z3 = (z1 + 2) % 4
    places = (z, z2, z1, z3)
    to_y = {"col": oc}
    to_k = {"grp": 2 * x + ok}
    to_x = {"grp": 2 * ox + k}
    to_xk = {"grp": 2 * ox + ok}
    to_z1 = {"row": z1}
    to_z2 = {"row": z2}
    tok = t_v.shape[0]
    share = g_v.shape[2]
    half = xl_v.shape[2]
    out_rows = u_v.shape[1]
    phases = ((c, 0, tok), (oc, 0, tok // 2), (oc, tok // 2, tok // 2))

    names = {}
    sends = []

    def copy(name, src, dst, where):
        i = names.setdefault(name, len(names))
        return pltpu.make_async_remote_copy(
            src_ref=src, dst_ref=dst, send_sem=send_sem.at[i], recv_sem=recv_sem.at[i],
            device_id=where, device_id_type=pl.DeviceIdType.MESH,
        )

    def send(name, src, dst, where):
        out = copy(name, src, dst, where)
        out.start()
        sends.append(out)

    def await_in(name, dst, where):
        copy(name, dst, dst, where).wait_recv()

    def load_a(block, sem):
        rows = pl.ds(pl.multiple_of(block * out_rows, out_rows), out_rows)
        return pltpu.make_async_copy(a_hbm.at[rows], a_v.at[rows], load_sem.at[sem])

    def load_g(part, sem):
        columns = pl.ds(pl.multiple_of(part * share, 128), share)
        return pltpu.make_async_copy(g_hbm.at[:, columns], g_v.at[part], load_sem.at[sem])

    odd = z % 2
    away_blocks = (1 - odd, 3 - odd)
    home_blocks = (odd, 2 + odd)
    loads = [
        pltpu.make_async_copy(t_hbm, t_v, load_sem.at[2]),
        load_a(away_blocks[0], 3),
        load_a(away_blocks[1], 4),
        pltpu.make_async_copy(c_hbm, c_v.at[c], load_sem.at[0]),
        load_g(z, 1),
        load_a(home_blocks[0], 5),
        load_a(home_blocks[1], 6),
    ] + [load_g((z + i) % 4, 6 + i) for i in range(1, 4)]
    for load in loads:
        load.start()

    barrier = pltpu.get_barrier_semaphore()
    partners = [to_y, to_k, to_x, to_xk, to_z1, to_z2]
    for where in partners:
        pl.semaphore_signal(barrier, inc=1, device_id=where, device_id_type=pl.DeviceIdType.MESH)
    pl.semaphore_wait(barrier, len(partners))

    def send_cot(ph):
        part = pl.ds(phases[ph][1], phases[ph][2])
        send(("cot", ph), c_hbm.at[part], c_v.at[c, part], to_y)

    send_cot(1)

    hot = lax.broadcasted_iota(jnp.int32, (tok, rows_ref.shape[1]), 0) + c * tok == rows_ref[...]
    oh_v[c] = jnp.where(hot, 1.0, 0.0).astype(BF16)
    send("hot", oh_v.at[c], oh_v.at[c], to_y)

    def pick(block, values):
        return lax.dot_general(oh_v[block], values, CONTRACT, preferred_element_type=F32).astype(BF16)

    def v_at(ph, core, side, step):
        block, first, count = phases[ph]
        row = pl.multiple_of(block * tok + first + (2 * core + side) * (count // 4), count // 4)
        return v_v.at[
            pl.ds(row, count // 4), pl.ds(pl.multiple_of(places[step] * share, 128), share)
        ]

    def cut(ph):
        return pl.ds(0, phases[ph][2] // 4)

    def product(ph):
        block, first, count = phases[ph]
        q = jnp.dot(c_v[block, first:first + count], g_v[z], preferred_element_type=F32)
        q_v[ph, :, cut(ph)] = q.reshape(4, count // 4, share)
        r1_s[ph, :, cut(ph)] = q_v[ph, pl.ds(2 * ok, 2), cut(ph)].astype(BF16)
        send(("r1", ph), r1_s.at[ph, :, cut(ph)], r1_r.at[ph, :, cut(ph)], to_k)

    def across(ph):
        await_in(("r1", ph), r1_r.at[ph, :, cut(ph)], to_k)
        r2_s[ph, cut(ph)] = (
            q_v[ph, 2 * k + ox, cut(ph)] + r1_r[ph, ox, cut(ph)].astype(F32)
        ).astype(BF16)
        send(("r2", ph), r2_s.at[ph, cut(ph)], r2_r.at[ph, cut(ph)], to_x)

    def finish(ph):
        await_in(("r2", ph), r2_r.at[ph, cut(ph)], to_x)
        total = (
            q_v[ph, 2 * k + x, cut(ph)] + r1_r[ph, x, cut(ph)].astype(F32)
            + r2_r[ph, cut(ph)].astype(F32)
        )
        mine = v_at(ph, k, x, 0)
        mine[...] = total.astype(BF16)
        send(("v", ph, 1), mine, mine, to_z2)
        send(("v", ph, 2), mine, mine, to_z1)
        send(("vx", ph, 0), mine, mine, to_x)
        send(("vk", ph, 0), mine, mine, to_k)

    def spread(ph, step):
        got = v_at(ph, k, x, step)
        await_in(("v", ph, step), got, to_z1)
        if step == 1:
            send(("v", ph, 3), got, got, to_z1)
        send(("vx", ph, step), got, got, to_x)
        send(("vk", ph, step), got, got, to_k)

    def relay(ph, step):
        got = v_at(ph, k, ox, step)
        await_in(("vx", ph, step), got, to_x)
        send(("vk", ph, 4 + step), got, got, to_k)

    def collect(ph):
        for step in range(4):
            await_in(("vk", ph, step), v_at(ph, ok, x, step), to_k)
        for step in range(4):
            await_in(("vk", ph, 4 + step), v_at(ph, ok, ox, step), to_k)

    def rows_b(ph, core):
        block, first, count = phases[ph]
        return pl.ds(pl.multiple_of(block * tok + first + core * (count // 2), count // 2), count // 2)

    def product_b(ph, j):
        block, first, count = phases[ph]
        unit = 4 * (ph - 1) + j
        q = jnp.dot(c_v[block, first:first + count], g_v[j], preferred_element_type=F32)
        qb_v[unit] = q.reshape(2, count // 2, share)
        b1_s[unit] = qb_v[unit, ok].astype(BF16)
        send(("b1", unit), b1_s.at[unit], b1_r.at[unit], to_k)

    def across_b(ph, j):
        unit = 4 * (ph - 1) + j
        await_in(("b1", unit), b1_r.at[unit], to_k)
        total = qb_v[unit, k] + b1_r[unit].astype(F32)
        qb_v[unit, k] = total
        b2_s[unit] = total.astype(BF16)
        send(("b2", unit), b2_s.at[unit], b2_r.at[unit], to_x)

    def finish_b(ph, j):
        unit = 4 * (ph - 1) + j
        await_in(("b2", unit), b2_r.at[unit], to_x)
        mine = v_v.at[rows_b(ph, k), j * share:(j + 1) * share]
        mine[...] = (qb_v[unit, k] + b2_r[unit].astype(F32)).astype(BF16)
        send(("bk", unit), mine, mine, to_k)

    def collect_b(ph):
        for j in range(4):
            got = v_v.at[rows_b(ph, ok), j * share:(j + 1) * share]
            await_in(("bk", 4 * (ph - 1) + j), got, to_k)

    def run_b(ph, between=None):
        for j in range(3):
            product_b(ph, j)
        across_b(ph, 0)
        product_b(ph, 3)
        if between:
            between()
        for j in range(1, 4):
            across_b(ph, j)

    def u_part(block):
        rows = a_v[pl.ds(pl.multiple_of(block * out_rows, out_rows), out_rows), :]
        return lax.dot_general(t_v[...], rows, (((1,), (1,)), ((), ())), preferred_element_type=F32)

    def at_half(ref, index):
        return ref.at[:, pl.ds(pl.multiple_of(index * half, 128), half)]

    def await_cot(ph):
        part = pl.ds(phases[ph][1], phases[ph][2])
        await_in(("cot", ph), c_v.at[oc, part], to_y)

    has_span = grp == z
    is_z2 = grp == z2
    is_z1 = grp == z1
    span = xs_v.at[c]
    x_z2 = copy("x2", span, span, to_z2)
    x_z1 = copy("x1", span, span, to_z1)

    loads[0].wait()
    px_v[...] = pick(c, t_v[...])

    @pl.when(has_span)
    def _():
        xs_v[c] = px_v[...]
        x_z2.start()
        x_z1.start()

    t_v[...] = t_v[...] * jnp.asarray(SHRINK, BF16)
    for i in range(2):
        loads[1 + i].wait()
        w_s[i] = u_part(away_blocks[i]).astype(BF16)
    send("w", w_s, w_r, to_z1)
    send_cot(2)
    loads[3].wait()
    loads[4].wait()
    product(0)
    ys_v[c] = pick(c, c_v[c])

    def y_copies(block):
        left = ys_v.at[block, :, pl.ds(pl.multiple_of(c * half, 128), half)]
        own = 0 if block is c else 1
        return left, [
            copy(("yl", own, i), left, yl_v.at[block], w) for i, w in enumerate([to_k, to_x, to_xk])
        ]

    left_c, y_c = y_copies(c)
    left_oc, y_oc = y_copies(oc)

    @pl.when(has_span)
    def _():
        for out in y_c:
            out.start()
        yl_v[c] = left_c[...]

    across(0)
    for i in range(2):
        loads[5 + i].wait()
        w_v[i] = u_part(home_blocks[i])
    finish(0)
    await_cot(1)
    for i in range(7, 10):
        loads[i].wait()
    run_b(1)

    @pl.when(is_z2)
    def _():
        x_z2.wait_recv()
        x_z1.start()

    await_in("w", w_r, to_z1)
    mine, away = z // 2, 1 - z // 2
    h_s[...] = (w_v[away] + w_r[away].astype(F32)).astype(BF16)
    send("h", h_s, h_r, to_z2)
    spread(0, 1)
    spread(0, 2)
    await_cot(2)
    run_b(2, lambda: spread(0, 3))
    for j in range(4):
        finish_b(1, j)
    send("xl", at_half(px_v, oc), xl_v.at[c], to_y)
    xl_v[c] = at_half(px_v, c)[...]

    @pl.when(jnp.logical_or(is_z1, grp == z3))
    def _():
        x_z1.wait_recv()

    send("xy", span, span, to_y)
    await_in("hot", oh_v.at[oc], to_y)
    ys_v[oc] = pick(oc, c_v[oc])

    @pl.when(has_span)
    def _():
        for out in y_oc:
            out.start()
        yl_v[oc] = left_oc[...]

    await_in("h", h_r, to_z2)
    u = w_v[mine] + w_r[mine].astype(F32) + h_r[...].astype(F32)
    u_v[c] = u.T.astype(BF16)
    send("u", u_v.at[c], u_v.at[c], to_y)
    for step in range(4):
        relay(0, step)
    for j in range(4):
        finish_b(2, j)
    collect(0)

    outs = []

    def put(src, dst):
        out = pltpu.make_async_copy(src, dst, out_sem.at[len(outs)])
        out.start()
        outs.append(out)

    def put_v(ph):
        block, first, count = phases[ph]
        rows = pl.ds(pl.multiple_of(block * tok + first, count), count)
        put(v_v.at[rows], v_out.at[rows])

    put_v(0)
    put(ys_v, ys_out)
    collect_b(1)
    put_v(1)
    await_in("xl", xl_v.at[oc], to_y)
    xlt_v[...] = xl_v[...].reshape(xlt_v.shape[::-1]).T
    put(xlt_v, xl_out)

    @pl.when(grp == 2 * (z // 2) + (1 - z % 2))
    def _():
        y_c[0].wait_recv()
        y_oc[0].wait_recv()

    @pl.when(grp == 2 * (1 - z // 2) + z % 2)
    def _():
        y_c[1].wait_recv()
        y_oc[1].wait_recv()

    @pl.when(grp == 2 * (1 - z // 2) + (1 - z % 2))
    def _():
        y_c[2].wait_recv()
        y_oc[2].wait_recv()

    ylt_v[...] = yl_v[...].reshape(ylt_v.shape[::-1]).T
    put(ylt_v, yl_out)
    await_in("xy", xs_v.at[oc], to_y)
    put(xs_v, xs_out)
    await_in("u", u_v.at[oc], to_y)
    for block in range(2):
        put(u_v.at[block], u_out.at[:, block * tok:(block + 1) * tok])
    collect_b(2)
    put_v(2)

    @pl.when(has_span)
    def _():
        x_z2.wait_send()
        x_z1.wait_send()
        for out in y_c + y_oc:
            out.wait_send()

    @pl.when(is_z2)
    def _():
        x_z1.wait_send()

    for out in sends:
        out.wait_send()
    for out in outs:
        out.wait()


def gather(rows, tokens_in, cotangent, act_inverse, grad_inverse, n_row):
    tok, feat = tokens_in.shape
    samples = rows.shape[1]
    share = grad_inverse.shape[1] // n_row
    out_rows = feat // n_row
    half = feat // 2
    piece = tok // 4
    v_shape, span = (2 * tok, grad_inverse.shape[1]), (2, samples, feat)
    left, left_t = (2, samples, half), (half, 2 * samples)
    shapes = [(out_rows, 2 * tok), v_shape, left_t, span, left_t, span]
    held = [(2, out_rows, tok), v_shape, left, span, left, span, left_t, left_t]
    vmem = pltpu.VMEM
    return pl.pallas_call(
        gather_kernel,
        out_shape=[vmem(s, BF16) for s in shapes],
        in_specs=[pl.BlockSpec(memory_space=vmem)] + [pl.BlockSpec(memory_space=pl.ANY)] * 4,
        out_specs=[pl.BlockSpec(memory_space=pl.ANY)] * 6,
        scratch_shapes=[
            vmem((tok, feat), BF16),
            vmem((2, tok, feat), BF16),
            vmem(act_inverse.shape, BF16),
            vmem((n_row, feat, share), BF16),
            vmem((2, tok, samples), BF16),
            vmem((samples, feat), BF16),
            vmem((1, 4, piece, share), F32),
            vmem((1, 2, piece, share), BF16),
            vmem((1, 2, piece, share), BF16),
            vmem((1, piece, share), BF16),
            vmem((1, piece, share), BF16),
            vmem((8, 2, piece, share), F32),
            vmem((8, piece, share), BF16),
            vmem((8, piece, share), BF16),
            vmem((8, piece, share), BF16),
            vmem((8, piece, share), BF16),
            vmem((2, tok, out_rows), BF16),
            vmem((2, tok, out_rows), BF16),
            vmem((2, tok, out_rows), F32),
            vmem((tok, out_rows), BF16),
            vmem((tok, out_rows), BF16),
        ] + [vmem(s, BF16) for s in held] + [
            pltpu.SemaphoreType.DMA((10,)),
            pltpu.SemaphoreType.DMA((9,)),
            pltpu.SemaphoreType.DMA((72,)),
            pltpu.SemaphoreType.DMA((72,)),
        ],
        compiler_params=pltpu.CompilerParams(
            collective_id=0, has_side_effects=True, vmem_limit_bytes=58 * 2 ** 20
        ),
        cost_estimate=pl.CostEstimate(flops=3 * 10 ** 9, bytes_accessed=10 ** 7, transcendentals=0),
    )(rows, tokens_in, cotangent, act_inverse, grad_inverse)


def product_kernel(total, ut, v, xt, xs, yt, ys, p_out, a_out, g_out):
    a_out[...] = jnp.dot(xt[...], xs[...], preferred_element_type=F32) * (1 / total)
    g_out[...] = jnp.dot(yt[...], ys[...], preferred_element_type=F32) * (1 / total)
    p_out[...] = jnp.dot(ut[...], v[...], preferred_element_type=F32) * (1 / SHRINK)


def products(ut, v, xt, xs, yt, ys):
    steps = 6
    total = xt.shape[1]

    def whole(a):
        return pl.BlockSpec(a.shape, lambda i: (0, 0))

    def cut(rows, width):
        return pl.BlockSpec((rows, width // steps), lambda i: (0, i))

    return pl.pallas_call(
        functools.partial(product_kernel, total),
        grid=(steps,),
        in_specs=[
            whole(ut), cut(v.shape[0], v.shape[1]),
            whole(xt), cut(total, xs.shape[1]), whole(yt), cut(total, ys.shape[1]),
        ],
        out_specs=[
            cut(ut.shape[0], v.shape[1]), cut(xt.shape[0], xs.shape[1]), cut(yt.shape[0], ys.shape[1])
        ],
        out_shape=[
            jax.ShapeDtypeStruct((ut.shape[0], v.shape[1]), F32),
            jax.ShapeDtypeStruct((xt.shape[0], xs.shape[1]), F32),
            jax.ShapeDtypeStruct((yt.shape[0], ys.shape[1]), F32),
        ],
        compiler_params=pltpu.CompilerParams(vmem_limit_bytes=40 * 2 ** 20),
        cost_estimate=pl.CostEstimate(flops=10 ** 9, bytes_accessed=17 * 10 ** 6, transcendentals=0),
    )(ut, v, xt, xs, yt, ys)


def flat(a):
    return a.reshape(-1, a.shape[-1])


def body_kernels(tokens_in, cotangent, sample_rows, act_inverse, grad_inverse):
    ut, v, xt, xs, yt, ys = gather(
        sample_rows[None], tokens_in, cotangent, act_inverse, grad_inverse, lax.axis_size("row")
    )
    return tuple(products(ut, v, xt, flat(xs), yt, flat(ys)))


def body(tokens_in, cotangent, sample_rows, act_inverse, grad_inverse):
    feat_row = tokens_in.shape[1]
    feat_grp = cotangent.shape[1]
    n_row = lax.axis_size("row")
    n_col = lax.axis_size("col")
    n_grp = lax.axis_size("grp")
    width = feat_row * n_row
    contract = (((0,), (0,)), ((), ()))
    col_index = lax.axis_index("col")
    grp_index = lax.axis_index("grp")
    row_index = lax.axis_index("row")
    small = tokens_in * jnp.asarray(SHRINK, tokens_in.dtype)
    part_u = lax.dot_general(
        small, act_inverse, (((1,), (1,)), ((), ())), preferred_element_type=jnp.float32
    )
    u = lax.psum_scatter(part_u.astype(jnp.bfloat16), "row", scatter_dimension=1, tiled=True)
    u = lax.all_gather(u, "col", axis=0, tiled=True)
    all_cot = lax.all_gather(cotangent, "col", axis=0, tiled=True)
    share = grad_inverse.shape[1] // n_row
    mine = lax.dynamic_slice_in_dim(grad_inverse, row_index * share, share, 1)
    part_v = jnp.dot(all_cot, mine, preferred_element_type=jnp.float32)
    v = lax.psum(part_v.astype(jnp.bfloat16), "grp")
    v = lax.all_gather(v, "row", axis=1, tiled=True)
    precond = lax.dot_general(u, v, contract, preferred_element_type=jnp.float32) * (1 / SHRINK)
    offsets = sample_rows - col_index * tokens_in.shape[0]
    picked_x = jnp.take(tokens_in, offsets, axis=0)
    picked_g = jnp.take(cotangent, offsets, axis=0)
    samples = picked_x.shape[0]
    total = samples * n_col
    act_panel = lax.all_gather(picked_x[None], ("row", "col"), axis=0, tiled=True).reshape(
        n_row, total, feat_row
    )
    grad_panel = lax.all_gather(picked_g[None], ("grp", "col"), axis=0, tiled=True).reshape(
        n_grp, total, feat_grp
    )
    tile = width // (n_row * n_col)
    first = (row_index * n_col + col_index) * tile
    act_left = lax.dynamic_slice(
        act_panel, (first // feat_row, 0, first % feat_row), (1, total, tile)
    )[0]
    per = feat_grp // feat_row
    act_span = lax.dynamic_slice_in_dim(act_panel, grp_index * per, per, 0)
    act_cov = jnp.einsum("sa,psf->apf", act_left, act_span, preferred_element_type=jnp.float32)
    act_cov = act_cov.reshape(tile, feat_grp) / total
    grad_left = lax.dynamic_slice(
        grad_panel, (first // feat_grp, 0, first % feat_grp), (1, total, tile)
    )[0]
    grad_span = lax.dynamic_index_in_dim(grad_panel, grp_index, 0, keepdims=False)
    grad_cov = (
        lax.dot_general(grad_left, grad_span, contract, preferred_element_type=jnp.float32) / total
    )
    return (precond, act_cov, grad_cov)


def solution(mesh):
    sizes = tuple(mesh.shape[name] for name in ("grp", "row", "col"))
    return jax.shard_map(
        body_kernels if sizes == (4, 4, 2) else body,
        mesh=mesh,
        in_specs=(P("col", "row"), P("col", "grp"), P("col"), P("grp", "row"), P("grp", "col")),
        out_specs=(P(("grp", "row"), "col"), P(("row", "col"), "grp"), P(("row", "col"), "grp")),
        check_vma=False,
    )
```
